32 devices in a mesh: groups: 2 (over x), blk: 8 (over z, y), chan: 2 (over core).
Axes of the slice: x: 2, y: 2, z: 4, core: 2. Of those that a mesh axis runs over, the one named last changes fastest.
Arguments:
- records: bfloat16 [1024, 2048], P('chan', ('groups', 'blk')), parts along dimension 1, as said below
- templates: bfloat16 [100, 2048, 1024], P(None, ('groups', 'blk'), 'chan'), parts along dimension 1, as said below
- offsets: int32 [2048, 1024], P(('groups', 'blk'), 'chan'), parts along dimension 0, may hold values from 0 to 4
- masks: int32 [2048, 1024], P(('groups', 'blk'), 'chan'), parts along dimension 0, may hold values 0 or 1
Outputs:
- detection: float32 [2048, 1024], P(('groups', 'blk'), 'chan'), parts along dimension 0
The draws below stay inside these ranges and needn't reach their ends.
There are 2 independent parts, one for each index of `groups`. The reference program is written for one: setup_inputs(seed, part) draws one part's arguments, and reference() takes and returns one part's arrays. A program takes and returns all parts, laid end to end along the dimension named above; each array names one. Nothing has to cross between parts.
Inputs may be any that keep to these rules, and one draw needn't show every extreme that they name: `records`: finite samples. `templates`: finite samples.
All inputs are finite; a program needn't handle non-finite values. No bound on the sum of `masks` on one device may be relied on, other than what follows from the above.
Results may differ from the reference program's by a relative error of at most 0.0041.
Values may be sent and summed in bfloat16 or wider, within the bound.
No kernel may reach another device: no remote copies, remote signals or barrier semaphores. Data moves between devices by JAX's collectives and lax.ppermute only.
A program may use at most 448 MiB of HBM per device.

```python
import jax
import jax.numpy as jnp
from jax import lax

C = 1024
K = 1024
L = 100
LE = 104
SEISMOGRAM_DELAY = 1024


def draw_records(key, part):
    key = jax.random.fold_in(key, 7)
    first, second, tertiary_subinterval = jax.random.split(key, 3)
    sensor_amplitude_factors = jnp.exp(jax.random.uniform(second, (C, 1), jnp.float32, 0.0, 2.4))
    tremor_arrivals = jnp.exp(jax.random.uniform(tertiary_subinterval, (1, SEISMOGRAM_DELAY // 16), jnp.float32, -1.0, 1.0))
    tremor_arrivals = jnp.repeat(tremor_arrivals, 16, axis=1)
    quiet_seismogram = jnp.clip(jax.random.normal(first, (C, SEISMOGRAM_DELAY), jnp.float32), -6.0, 6.0)
    return (quiet_seismogram * sensor_amplitude_factors * tremor_arrivals).astype(jnp.bfloat16)


def draw_templates(key, part):
    key = jax.random.fold_in(key, 13)
    first, second = jax.random.split(key, 2)
    scales = jnp.exp(jax.random.uniform(second, (1, K, C), jnp.float32, 0.0, 2.3))
    quiet_seismogram = jnp.clip(jax.random.normal(first, (L, K, C), jnp.float32), -6.0, 6.0)
    return (quiet_seismogram * scales).astype(jnp.bfloat16)


def with_ends(drawn, rng, smallest, top_value):
    longest = drawn.shape.index(max(drawn.shape))
    spots = []
    for shift in (0, 1):
        where = [jax.random.randint(jax.random.fold_in(rng, axis), (), 0, length) for axis, length in enumerate(drawn.shape)]
        where[longest] = (where[longest] + shift) % drawn.shape[longest]
        spots.append(tuple(where))
    return drawn.at[spots[0]].set(smallest).at[spots[1]].set(top_value)


def setup_inputs(seed: int = 0, part: int = 0) -> dict:
    arg_keys = jax.random.split(jax.random.key(seed), 5)
    own_keys = jax.random.split(jax.random.fold_in(arg_keys[4], part), 5)
    return {
        "records": draw_records(jax.random.fold_in(jax.random.fold_in(arg_keys[4], part), 71), part),
        "templates": draw_templates(jax.random.fold_in(jax.random.fold_in(arg_keys[4], part), 71), part),
        "offsets": with_ends(jax.random.randint(own_keys[2], (K, C), 0, LE - L + 1), jax.random.fold_in(own_keys[2], 1), 0, LE - L).astype(jnp.int32),
        "masks": with_ends((jax.random.randint(own_keys[3], (K, C), 0, 4) < 3).astype(jnp.int32), jax.random.fold_in(own_keys[3], 1), 0, 1),
    }


EPS = 1e-06

def window_inverse(zero_extended_signal):
    square = zero_extended_signal * zero_extended_signal
    zero = jnp.zeros((), square.dtype)
    dims = (1,) * (square.ndim - 1) + (LE,)
    strides = (1,) * square.ndim
    total = lax.reduce_window(square, zero, lax.add, dims, strides, 'VALID')
    return lax.rsqrt(total / LE + EPS)

def unfold_lags(segment, width):
    length = segment.shape[-1]
    tiled = jnp.tile(segment, (1,) * (segment.ndim - 1) + (LE + 1,))
    cut = tiled[..., :LE * (length + 1)]
    return cut.reshape(segment.shape[:-1] + (LE, length + 1))[..., :width]

def embed_templates(templates, offsets, masks):
    tfloat = templates.astype(jnp.float32)
    tinv = lax.rsqrt(lax.optimization_barrier(jnp.mean(tfloat * tfloat, axis=0)) + EPS)
    scale = tinv * masks.astype(jnp.float32) / L
    scaled = tfloat * scale[None]
    embedded = jnp.zeros((LE,) + scaled.shape[1:], jnp.float32)
    for delay_amount in range(LE - L + 1):
        moved = jnp.pad(scaled, ((delay_amount, LE - L - delay_amount), (0, 0), (0, 0)))
        embedded = embedded + jnp.where((offsets == delay_amount)[None], moved, 0.0)
    embedded = embedded.astype(jnp.bfloat16)
    return jnp.transpose(embedded, (1, 2, 0)).reshape(scaled.shape[1], -1)

def window_matrix(segment, width):
    wide = segment.astype(jnp.float32)
    inverse = window_inverse(wide)
    shifted = unfold_lags(segment, width).astype(jnp.float32)
    windows = (shifted * inverse[..., None, :]).astype(jnp.bfloat16)
    return windows.reshape(segment.shape[:-2] + (segment.shape[-2] * LE, width))

def reference(records, templates, offsets, masks):
    flat = embed_templates(templates, offsets, masks)
    zero_extended_signal = jnp.concatenate([records, jnp.zeros((C, LE - 1), records.dtype)], axis=1)
    block = 512

    def one_block(index):
        segment = lax.dynamic_slice_in_dim(zero_extended_signal, index * block, block + LE - 1, 1)
        return jnp.dot(flat, window_matrix(segment, block), preferred_element_type=jnp.float32)
    blocks = lax.map(one_block, jnp.arange(SEISMOGRAM_DELAY // block, dtype=jnp.int32))
    return jnp.transpose(blocks, (1, 0, 2)).reshape(K, SEISMOGRAM_DELAY)
```

```python
import functools

import jax
import jax.numpy as jnp
from jax import lax
from jax.experimental import pallas as pl
from jax.experimental.pallas import tpu as pltpu
from jax.sharding import PartitionSpec as P

L = 100
LE = 104
SPAN = LE - L
EPS = 1e-06
LANES = 128
TAPS = 8
GROUP = 8
VMEM = 56 * 1024 * 1024


def embed_kernel(t_ref, off_ref, mask_ref, e_ref):
    rows, cols = off_ref.shape

    def square(l, acc):
        v = t_ref[l].astype(jnp.float32)
        return acc + v * v

    total = lax.fori_loop(0, L, square, jnp.zeros((rows, cols), jnp.float32), unroll=4)
    scale = lax.rsqrt(total / L + EPS) * mask_ref[...].astype(jnp.float32) / L
    off = off_ref[...].astype(jnp.float32).astype(jnp.bfloat16)
    zero = jnp.zeros((rows, cols), jnp.bfloat16)

    def place(j, read):
        value = read(j)
        for d in range(1, SPAN + 1):
            value = jnp.where(off == d, read(j - d), value)
        scaled = value.astype(jnp.float32) * scale
        e_ref[j] = scaled.T.astype(jnp.bfloat16)

    def edge(l):
        return t_ref[l] if 0 <= l < L else zero

    for j in range(SPAN):
        place(j, edge)
    for j in range(L, LE):
        place(j, edge)

    def body(j, carry):
        place(j, lambda l: t_ref[l])
        return carry

    lax.fori_loop(SPAN, L, body, 0, unroll=2)


def embed(templates, offsets, masks, start, width):
    k = offsets.shape[0]
    first = start // LANES
    steps = width // LANES
    return pl.pallas_call(
        embed_kernel,
        grid=(steps,),
        in_specs=[
            pl.BlockSpec((L, k, LANES), lambda i: (0, 0, first + i)),
            pl.BlockSpec((k, LANES), lambda i: (0, first + i)),
            pl.BlockSpec((k, LANES), lambda i: (0, first + i)),
        ],
        out_specs=pl.BlockSpec((LE, LANES, k), lambda i: (0, i, 0)),
        out_shape=jax.ShapeDtypeStruct((LE, width, k), jnp.bfloat16),
        compiler_params=pltpu.CompilerParams(vmem_limit_bytes=VMEM),
        cost_estimate=pl.CostEstimate(
            flops=20 * LE * width * k, bytes_accessed=2 * 2 * LE * width * k, transcendentals=0
        ),
    )(templates, offsets, masks)


def ring_position(b, n):
    z, y = b // 2, b % 2
    return z * (1 - y) + (n - 1 - z) * y


def ring_block(p, n):
    half = n // 2
    low = (p < half) * 1 if isinstance(p, int) else (p < half).astype(jnp.int32)
    return low * (2 * p) + (1 - low) * (2 * (n - 1 - p) + 1)


def ring_gather(x, n, forward_last):
    order = [ring_block(p, n) for p in range(n)]
    up = [(order[p], order[(p + 1) % n]) for p in range(n)]
    down = [(order[(p + 1) % n], order[p]) for p in range(n)]
    half = n // 2
    blocks = {0: x}
    a = b = x
    for step in range(1, half + 1):
        if step < half or forward_last:
            a = lax.ppermute(a, "blk", up)
            blocks[(-step) % n] = a
        if step < half or not forward_last:
            b = lax.ppermute(b, "blk", down)
            blocks[step] = b
    return [blocks[d] for d in range(n)]


def prepare(n, block_refs, flat_ref, x_ref, g_ref, n_ref):
    lags, width = block_refs[0].shape
    me = ring_position(lax.axis_index("blk"), n)
    for d in range(n):
        where = ring_block(lax.rem(me + d, n), n)
        for w in range(width // LANES):
            flat_ref[w, pl.ds(pl.multiple_of(where * lags, lags), lags), :] = block_refs[d][
                :, w * LANES : (w + 1) * LANES
            ].astype(jnp.float32)
    for w in range(width // LANES):
        flat_ref[w, n * lags :, :] = jnp.zeros((lags, LANES), jnp.float32)

    groups = (lags + LE) // GROUP

    def spread(g, carry):
        sums = [None] * (width // LANES)
        for r in range(GROUP):
            u = g * GROUP + r
            for w in range(width // LANES):
                value = flat_ref[w, pl.ds(u, n, stride=lags), :]
                x_ref[u, :, w * LANES : (w + 1) * LANES] = value
                square = value * value
                sums[w] = square if r == 0 else sums[w] + square
        for w in range(width // LANES):
            g_ref[g, :, w * LANES : (w + 1) * LANES] = sums[w]
        return carry

    lax.fori_loop(0, groups, spread, 0)

    def norms(g, carry):
        middle = g_ref[g + 1]
        for i in range(2, LE // GROUP):
            middle = middle + g_ref[g + i]
        tails = [None] * GROUP
        tail = None
        for r in range(GROUP - 1, -1, -1):
            value = x_ref[g * GROUP + r]
            square = value * value
            tail = square if tail is None else tail + square
            tails[r] = tail
        head = None
        for r in range(GROUP):
            total = middle + tails[r]
            if r > 0:
                value = x_ref[g * GROUP + LE + r - 1]
                square = value * value
                head = square if head is None else head + square
                total = total + head
            n_ref[g * GROUP + r] = lax.rsqrt(total / LE + EPS)
        return carry

    lax.fori_loop(0, lags // GROUP, norms, 0)


def correlate_kernel(n, steps, carried, *refs):
    blocks = refs[:n]
    e_ref = refs[n]
    rest = refs[n + 1 :]
    if carried:
        before_ref, mine_ref, other_ref, acc_ref, flat_ref, x_ref, g_ref, n_ref = rest
    else:
        acc_ref, flat_ref, x_ref, g_ref, n_ref = rest
    lags, width = blocks[0].shape
    k = e_ref.shape[-1]
    step = pl.program_id(0)

    @pl.when(step == 0)
    def _():
        prepare(n, blocks, flat_ref, x_ref, g_ref, n_ref)
        if carried:
            acc_ref[...] = before_ref[...]
        else:
            acc_ref[...] = jnp.zeros_like(acc_ref)

    chunk = 256 // n
    weights = e_ref[...].reshape(TAPS * width, k)

    def tile(m, carry):
        u = m * chunk
        norm = n_ref[pl.ds(u, chunk)]
        parts = []
        for tap in range(TAPS):
            value = x_ref[pl.ds(u + step * TAPS + tap, chunk)] * norm
            parts.append(value.reshape(chunk * n, width).astype(jnp.bfloat16))
        windows = jnp.concatenate(parts, axis=1)
        rows = pl.ds(pl.multiple_of(m * chunk * n, chunk * n), chunk * n)
        acc_ref[rows, :] += jnp.dot(windows, weights, preferred_element_type=jnp.float32)
        return carry

    lax.fori_loop(0, lags // chunk, tile, 0)

    if carried:

        @pl.when(step == steps - 1)
        def _():
            core = lax.axis_index("chan")
            half = n // 2
            for out_ref, first in ((mine_ref, core * half), (other_ref, (1 - core) * half)):
                for v in range(half):
                    value = acc_ref[pl.ds(first + v, lags, stride=n), :]
                    out_ref[:, v * lags : (v + 1) * lags] = value.T


def correlate(blocks, embedded, before):
    n = len(blocks)
    lags, width = blocks[0].shape
    k = embedded.shape[-1]
    steps = LE // TAPS
    whole = pl.BlockSpec(memory_space=pltpu.VMEM)
    carried = before is not None
    in_specs = [whole] * n + [pl.BlockSpec((TAPS, width, k), lambda i: (i, 0, 0))]
    scratch = [
        pltpu.VMEM((width // LANES, (n + 1) * lags, LANES), jnp.float32),
        pltpu.VMEM((lags + LE, n, width), jnp.float32),
        pltpu.VMEM(((lags + LE) // GROUP, n, width), jnp.float32),
        pltpu.VMEM((lags, n, width), jnp.float32),
    ]
    args = list(blocks) + [embedded]
    if carried:
        in_specs.append(whole)
        args.append(before)
        out_specs = [whole, whole]
        out_shape = [jax.ShapeDtypeStruct((k, n * lags // 2), jnp.float32)] * 2
        scratch = [pltpu.VMEM((n * lags, k), jnp.float32)] + scratch
    else:
        out_specs = whole
        out_shape = jax.ShapeDtypeStruct((n * lags, k), jnp.float32)
    return pl.pallas_call(
        functools.partial(correlate_kernel, n, steps, carried),
        grid=(steps,),
        in_specs=in_specs,
        out_specs=out_specs,
        out_shape=out_shape,
        scratch_shapes=scratch,
        compiler_params=pltpu.CompilerParams(vmem_limit_bytes=VMEM),
        cost_estimate=pl.CostEstimate(
            flops=2 * n * lags * LE * width * k,
            bytes_accessed=2 * LE * width * k,
            transcendentals=0,
        ),
    )(*args)


def per_device(n, records, templates, offsets, masks):
    channels = records.shape[0]
    half = channels // 2
    turned = records.T
    first = ring_gather(turned[:, :half], n, True)
    second = ring_gather(turned[:, half:], n, False)
    first_weights = embed(templates, offsets, masks, 0, half)
    second_weights = embed(templates, offsets, masks, half, half)
    partial_sum = correlate(first, first_weights, None)
    mine, other = correlate(second, second_weights, partial_sum)
    return mine + lax.ppermute(other, "chan", [(0, 1), (1, 0)])


def solution(mesh):
    return jax.shard_map(
        functools.partial(per_device, mesh.shape["blk"]),
        mesh=mesh,
        in_specs=(
            P("chan", ("groups", "blk")),
            P(None, ("groups", "blk"), "chan"),
            P(("groups", "blk"), "chan"),
            P(("groups", "blk"), "chan"),
        ),
        out_specs=P(("groups", "blk"), "chan"),
        check_vma=False,
    )
```

```python
import functools

import jax
import jax.numpy as jnp
from jax import lax
from jax.experimental import pallas as pl
from jax.experimental.pallas import tpu as pltpu
from jax.sharding import PartitionSpec as P

L = 100
LE = 104
SPAN = LE - L
EPS = 1e-06
LANES = 128
PIECES = 4
ROWS = 16
TAPS = 4
TILE = 512
GROUP = 8
VMEM = 56 * 1024 * 1024


def embed_kernel(t_ref, off_ref, mask_ref, e_ref):
    rows, cols = off_ref.shape

    def square(l, acc):
        v = t_ref[l].astype(jnp.float32)
        return acc + v * v

    total = lax.fori_loop(0, L, square, jnp.zeros((rows, cols), jnp.float32), unroll=4)
    scale = lax.rsqrt(total / L + EPS) * mask_ref[...].astype(jnp.float32) / L
    off = off_ref[...].astype(jnp.float32).astype(jnp.bfloat16)
    zero = jnp.zeros((rows, cols), jnp.bfloat16)

    def place(j, read):
        value = read(j)
        for d in range(1, SPAN + 1):
            value = jnp.where(off == d, read(j - d), value)
        e_ref[j] = (value.astype(jnp.float32) * scale).astype(jnp.bfloat16)

    def edge(l):
        return t_ref[l] if 0 <= l < L else zero

    for j in range(SPAN):
        place(j, edge)
    for j in range(L, LE):
        place(j, edge)

    def body(j, carry):
        place(j, lambda l: t_ref[l])
        return carry

    lax.fori_loop(SPAN, L, body, 0, unroll=4)


def embed(templates, offsets, masks, piece):
    k, channels = offsets.shape
    rows = k // PIECES
    steps = rows // ROWS
    first = piece * steps
    return pl.pallas_call(
        embed_kernel,
        grid=(steps,),
        in_specs=[
            pl.BlockSpec((L, ROWS, channels), lambda i: (0, first + i, 0)),
            pl.BlockSpec((ROWS, channels), lambda i: (first + i, 0)),
            pl.BlockSpec((ROWS, channels), lambda i: (first + i, 0)),
        ],
        out_specs=pl.BlockSpec((LE, ROWS, channels), lambda i: (0, i, 0)),
        out_shape=jax.ShapeDtypeStruct((LE, rows, channels), jnp.bfloat16),
        compiler_params=pltpu.CompilerParams(vmem_limit_bytes=VMEM),
        cost_estimate=pl.CostEstimate(
            flops=20 * LE * rows * channels,
            bytes_accessed=2 * 2 * LE * rows * channels,
            transcendentals=0,
        ),
    )(templates, offsets, masks)


def ring_position(b, n):
    z, y = b // 2, b % 2
    return z * (1 - y) + (n - 1 - z) * y


def ring_block(p, n):
    half = n // 2
    low = (p < half) * 1 if isinstance(p, int) else (p < half).astype(jnp.int32)
    return low * (2 * p) + (1 - low) * (2 * (n - 1 - p) + 1)


def ring_gather(x, n):
    order = [ring_block(p, n) for p in range(n)]
    up = [(order[p], order[(p + 1) % n]) for p in range(n)]
    down = [(order[(p + 1) % n], order[p]) for p in range(n)]
    blocks = {0: x}
    a = b = x
    for step in range(1, n // 2 + 1):
        a = lax.ppermute(a, "blk", up)
        blocks[n - step] = a
        if step < n // 2:
            b = lax.ppermute(b, "blk", down)
            blocks[step] = b
    return [blocks[d] for d in range(n)]


def prepare(n, block_refs, flat_ref, x_ref, g_ref, n_ref):
    lags, width = block_refs[0].shape
    me = ring_position(lax.axis_index("blk"), n)
    for d in range(n):
        where = ring_block(lax.rem(me + d, n), n)
        for w in range(width // LANES):
            flat_ref[w, pl.ds(pl.multiple_of(where * lags, lags), lags), :] = block_refs[d][
                :, w * LANES : (w + 1) * LANES
            ].astype(jnp.float32)
    for w in range(width // LANES):
        flat_ref[w, n * lags :, :] = jnp.zeros((lags, LANES), jnp.float32)

    groups = (lags + LE) // GROUP

    def spread(g, carry):
        sums = [None] * (width // LANES)
        for r in range(GROUP):
            u = g * GROUP + r
            for w in range(width // LANES):
                value = flat_ref[w, pl.ds(u, n, stride=lags), :]
                x_ref[u, :, w * LANES : (w + 1) * LANES] = value
                square = value * value
                sums[w] = square if r == 0 else sums[w] + square
        for w in range(width // LANES):
            g_ref[g, :, w * LANES : (w + 1) * LANES] = sums[w]
        return carry

    lax.fori_loop(0, groups, spread, 0)
    x_ref[lags + LE :] = jnp.zeros((2 * TAPS, n, width), jnp.float32)

    def norms(g, carry):
        middle = g_ref[g + 1]
        for i in range(2, LE // GROUP):
            middle = middle + g_ref[g + i]
        tails = [None] * GROUP
        tail = None
        for r in range(GROUP - 1, -1, -1):
            value = x_ref[g * GROUP + r]
            square = value * value
            tail = square if tail is None else tail + square
            tails[r] = tail
        head = None
        for r in range(GROUP):
            total = middle + tails[r]
            if r > 0:
                value = x_ref[g * GROUP + LE + r - 1]
                square = value * value
                head = square if head is None else head + square
                total = total + head
            n_ref[g * GROUP + r] = lax.rsqrt(total / LE + EPS)
        return carry

    lax.fori_loop(0, lags // GROUP, norms, 0)


def build(x_ref, n_ref, w_ref, n, tap0, m):
    width = x_ref.shape[-1]
    for u8 in range(TILE // (n * 8)):
        u = m * (TILE // n) + u8 * 8
        rows = pl.ds(pl.multiple_of(u * n, 8 * n), 8 * n)
        for w in range(width // LANES):
            lanes = slice(w * LANES, (w + 1) * LANES)
            norm = n_ref[pl.ds(u, 8), :, lanes]
            xs = x_ref[pl.ds(u + tap0, TAPS + 7), :, lanes]
            for tap in range(TAPS):
                value = (xs[tap : tap + 8] * norm).reshape(8 * n, LANES).astype(jnp.bfloat16)
                w_ref[rows, tap * width + w * LANES : tap * width + (w + 1) * LANES] = value


def correlate_kernel(n, steps, *refs):
    blocks = refs[:n]
    e_refs = refs[n : n + PIECES]
    mine_ref, other_ref, acc_ref, flat_ref, x_ref, g_ref, n_ref, even_ref, odd_ref = refs[n + PIECES :]
    lags, width = blocks[0].shape
    tiles = n * lags // TILE
    step = pl.program_id(0)

    @pl.when(step == 0)
    def _():
        prepare(n, blocks, flat_ref, x_ref, g_ref, n_ref)
        acc_ref[...] = jnp.zeros_like(acc_ref)

        def first(m, carry):
            build(x_ref, n_ref, even_ref, n, 0, m)
            return carry

        lax.fori_loop(0, tiles, first, 0)

    def advance(now_ref, later_ref, part, tap0):
        weights = jnp.concatenate(
            [
                jnp.concatenate([e_ref[part * TAPS + tap] for e_ref in e_refs], axis=0)
                for tap in range(TAPS)
            ],
            axis=1,
        )

        def tile(m, carry):
            rows = pl.ds(pl.multiple_of(m * TILE, TILE), TILE)
            acc_ref[rows, :] += lax.dot_general(
                now_ref[rows, :],
                weights,
                (((1,), (1,)), ((), ())),
                preferred_element_type=jnp.float32,
            )
            build(x_ref, n_ref, later_ref, n, tap0, m)
            return carry

        lax.fori_loop(0, tiles, tile, 0)

    advance(even_ref, odd_ref, 0, step * 2 * TAPS + TAPS)
    advance(odd_ref, even_ref, 1, step * 2 * TAPS + 2 * TAPS)

    @pl.when(step == steps - 1)
    def _():
        core = lax.axis_index("chan")
        half = n // 2
        for out_ref, first in ((mine_ref, core * half), (other_ref, (1 - core) * half)):
            for v in range(half):
                value = acc_ref[pl.ds(first + v, lags, stride=n), :]
                out_ref[:, v * lags : (v + 1) * lags] = value.T


def correlate(blocks, pieces):
    n = len(blocks)
    lags, width = blocks[0].shape
    k = PIECES * pieces[0].shape[1]
    steps = LE // (2 * TAPS)
    whole = pl.BlockSpec(memory_space=pltpu.VMEM)
    e_spec = pl.BlockSpec((2 * TAPS, k // PIECES, width), lambda i: (i, 0, 0))
    return pl.pallas_call(
        functools.partial(correlate_kernel, n, steps),
        grid=(steps,),
        in_specs=[whole] * n + [e_spec] * PIECES,
        out_specs=[whole, whole],
        out_shape=[jax.ShapeDtypeStruct((k, n * lags // 2), jnp.float32)] * 2,
        scratch_shapes=[
            pltpu.VMEM((n * lags, k), jnp.float32),
            pltpu.VMEM((width // LANES, (n + 1) * lags, LANES), jnp.float32),
            pltpu.VMEM((lags + LE + 2 * TAPS, n, width), jnp.float32),
            pltpu.VMEM(((lags + LE) // GROUP, n, width), jnp.float32),
            pltpu.VMEM((lags, n, width), jnp.float32),
            pltpu.VMEM((n * lags, TAPS * width), jnp.bfloat16),
            pltpu.VMEM((n * lags, TAPS * width), jnp.bfloat16),
        ],
        compiler_params=pltpu.CompilerParams(vmem_limit_bytes=VMEM),
        cost_estimate=pl.CostEstimate(
            flops=2 * n * lags * LE * width * k,
            bytes_accessed=2 * LE * width * k,
            transcendentals=0,
        ),
    )(*blocks, *pieces)


def per_device(n, records, templates, offsets, masks):
    blocks = ring_gather(records.T, n)
    pieces = [embed(templates, offsets, masks, piece) for piece in range(PIECES)]
    mine, other = correlate(blocks, pieces)
    return mine + lax.ppermute(other, "chan", [(0, 1), (1, 0)])


def solution(mesh):
    return jax.shard_map(
        functools.partial(per_device, mesh.shape["blk"]),
        mesh=mesh,
        in_specs=(
            P("chan", ("groups", "blk")),
            P(None, ("groups", "blk"), "chan"),
            P(("groups", "blk"), "chan"),
            P(("groups", "blk"), "chan"),
        ),
        out_specs=P(("groups", "blk"), "chan"),
        check_vma=False,
    )
```

```python
import functools

import jax
import jax.numpy as jnp
from jax import lax
from jax.experimental import pallas as pl
from jax.experimental.pallas import tpu as pltpu
from jax.sharding import PartitionSpec as P

L = 100
LE = 104
SPAN = LE - L
EPS = 1e-06
LANES = 128
PIECES = 4
ROWS = 16
TAPS = 4
TILE = 512
GROUP = 8
VMEM = 56 * 1024 * 1024


def embed_kernel(t_ref, off_ref, mask_ref, e_ref):
    rows, cols = off_ref.shape
    for w in range(cols // LANES):
        lanes = slice(w * LANES, (w + 1) * LANES)
        total = jnp.zeros((rows, LANES), jnp.float32)
        for l in range(L):
            v = t_ref[l, :, lanes].astype(jnp.float32)
            total = total + v * v
        scale = lax.rsqrt(total / L + EPS) * mask_ref[:, lanes].astype(jnp.float32) / L
        off = off_ref[:, lanes]
        odd = ((off & 1) == 1).astype(jnp.bfloat16) > 0
        high = (off >= 2).astype(jnp.bfloat16) > 0
        full = (off == SPAN).astype(jnp.bfloat16) > 0
        zero = jnp.zeros((rows, LANES), jnp.bfloat16)
        plain = [zero] * SPAN
        moved = [zero] * 2
        for j in range(LE):
            sample = t_ref[j, :, lanes] if j < L else zero
            now = jnp.where(odd, plain[-1], sample)
            value = jnp.where(full, plain[0], jnp.where(high, moved[0], now))
            e_ref[j, :, lanes] = (value.astype(jnp.float32) * scale).astype(jnp.bfloat16)
            plain = plain[1:] + [sample]
            moved = moved[1:] + [now]


def embed(templates, offsets, masks, piece):
    k, channels = offsets.shape
    rows = k // PIECES
    steps = rows // ROWS
    first = piece * steps
    width = 2 * LANES
    return pl.pallas_call(
        embed_kernel,
        grid=(steps, channels // width),
        in_specs=[
            pl.BlockSpec((L, ROWS, width), lambda i, j: (0, first + i, j)),
            pl.BlockSpec((ROWS, width), lambda i, j: (first + i, j)),
            pl.BlockSpec((ROWS, width), lambda i, j: (first + i, j)),
        ],
        out_specs=pl.BlockSpec((LE, ROWS, width), lambda i, j: (0, i, j)),
        out_shape=jax.ShapeDtypeStruct((LE, rows, channels), jnp.bfloat16),
        compiler_params=pltpu.CompilerParams(vmem_limit_bytes=VMEM),
        cost_estimate=pl.CostEstimate(
            flops=20 * LE * rows * channels,
            bytes_accessed=2 * 2 * LE * rows * channels,
            transcendentals=0,
        ),
    )(templates, offsets, masks)


def ring_position(b, n):
    z, y = b // 2, b % 2
    return z * (1 - y) + (n - 1 - z) * y


def ring_block(p, n):
    half = n // 2
    low = (p < half) * 1 if isinstance(p, int) else (p < half).astype(jnp.int32)
    return low * (2 * p) + (1 - low) * (2 * (n - 1 - p) + 1)


def ring_gather(x, n, beside):
    order = [ring_block(p, n) for p in range(n)]
    up = [(order[p], order[(p + 1) % n]) for p in range(n)]
    down = [(order[(p + 1) % n], order[p]) for p in range(n)]
    blocks = {0: x}
    done = []
    a = b = x
    for step in range(1, n // 2 + 1):
        a = lax.ppermute(a, "blk", up)
        if step < n // 2:
            b = lax.ppermute(b, "blk", down)
        if step <= PIECES:
            done.append(beside(step - 1))
            a, b, done[-1] = lax.optimization_barrier((a, b, done[-1]))
        blocks[n - step] = a
        if step < n // 2:
            blocks[step] = b
    return [blocks[d] for d in range(n)], done


def prepare(n, block_refs, x_ref, g_ref, n_ref):
    lags, width = block_refs[0].shape
    me = ring_position(lax.axis_index("blk"), n)
    for d in range(n):
        v = ring_block(lax.rem(me + d, n), n)
        for w in range(width // LANES):
            for u in range(0, lags, 16):
                value = block_refs[d][u : u + 16, w * LANES : (w + 1) * LANES].astype(jnp.float32)
                for i in range(2):
                    x_ref[w, pl.ds((u + 8 * i) * n + v, 8, stride=n), :] = value[8 * i : 8 * i + 8]

        @pl.when(v > 0)
        def _():
            for w in range(width // LANES):
                for u in range(0, LE, 8):
                    value = x_ref[w, pl.ds(u * n + v, 8, stride=n), :]
                    x_ref[w, pl.ds((lags + u) * n + v - 1, 8, stride=n), :] = value

        @pl.when(v == 0)
        def _():
            for w in range(width // LANES):
                for u in range(0, LE, 8):
                    x_ref[w, pl.ds((lags + u) * n + n - 1, 8, stride=n), :] = jnp.zeros(
                        (8, LANES), jnp.float32
                    )

    x_ref[:, (lags + LE) * n :, :] = jnp.zeros((width // LANES, 2 * TAPS * n, LANES), jnp.float32)
    size = GROUP * n

    def energy(g, carry):
        for w in range(width // LANES):
            value = x_ref[w, pl.ds(pl.multiple_of(g * size, size), size), :].reshape(GROUP, n, LANES)
            g_ref[w, g] = jnp.sum(value * value, axis=0)
        return carry

    lax.fori_loop(0, (lags + LE) // GROUP, energy, 0)

    def norms(g, carry):
        for w in range(width // LANES):
            middle = g_ref[w, g + 1]
            for i in range(2, LE // GROUP):
                middle = middle + g_ref[w, g + i]
            left = x_ref[w, pl.ds(pl.multiple_of(g * size, size), size), :].reshape(GROUP, n, LANES)
            right = x_ref[w, pl.ds(pl.multiple_of(g * size + LE * n, size), size), :]
            right = right.reshape(GROUP, n, LANES)
            left = left * left
            right = right * right
            tails = [None] * GROUP
            tail = middle
            for r in range(GROUP - 1, -1, -1):
                tail = tail + left[r]
                tails[r] = tail
            head = None
            for r in range(GROUP):
                total = tails[r]
                if r > 0:
                    head = right[0] if r == 1 else head + right[r - 1]
                    total = total + head
                row = pl.ds(pl.multiple_of((g * GROUP + r) * n, n), n)
                n_ref[w, row, :] = lax.rsqrt(total / LE + EPS)
        return carry

    lax.fori_loop(0, lags // GROUP, norms, 0)


def build(x_ref, n_ref, w_ref, n, tap0, m):
    tiles = x_ref.shape[0]
    size = 8 * n
    for i in range(TILE // size):
        row = m * TILE + i * size
        rows = pl.ds(pl.multiple_of(row, size), size)
        for w in range(tiles):
            norm = n_ref[w, rows, :]
            xs = x_ref[w, pl.ds(pl.multiple_of(row + tap0 * n, n), (TAPS + 7) * n), :]
            for tap in range(TAPS):
                value = (xs[tap * n : tap * n + size] * norm).astype(jnp.bfloat16)
                w_ref[rows, (tap * tiles + w) * LANES : (tap * tiles + w + 1) * LANES] = value


def correlate_kernel(n, steps, *refs):
    blocks = refs[:n]
    e_refs = refs[n : n + PIECES]
    mine_ref, other_ref, acc0_ref, acc1_ref, x_ref, g_ref, n_ref, even_ref, odd_ref = refs[n + PIECES :]
    lags, width = blocks[0].shape
    tiles = n * lags // TILE
    step = pl.program_id(0)

    @pl.when(step == 0)
    def _():
        prepare(n, blocks, x_ref, g_ref, n_ref)
        acc0_ref[...] = jnp.zeros_like(acc0_ref)
        acc1_ref[...] = jnp.zeros_like(acc1_ref)

        def first(m, carry):
            build(x_ref, n_ref, even_ref, n, 0, m)
            return carry

        lax.fori_loop(0, tiles, first, 0)

    def advance(now_ref, later_ref, part, tap0):
        weights = jnp.concatenate(
            [
                jnp.concatenate([e_ref[part * TAPS + tap] for e_ref in e_refs], axis=0)
                for tap in range(TAPS)
            ],
            axis=1,
        )

        def tile(m, carry):
            rows = pl.ds(pl.multiple_of(m * TILE, TILE), TILE)
            half = TAPS * width // 2
            for acc_ref, part in ((acc0_ref, slice(0, half)), (acc1_ref, slice(half, 2 * half))):
                acc_ref[rows, :] += lax.dot_general(
                    now_ref[rows, part],
                    weights[:, part],
                    (((1,), (1,)), ((), ())),
                    preferred_element_type=jnp.float32,
                )
            build(x_ref, n_ref, later_ref, n, tap0, m)
            return carry

        lax.fori_loop(0, tiles, tile, 0)

    advance(even_ref, odd_ref, 0, step * 2 * TAPS + TAPS)
    advance(odd_ref, even_ref, 1, step * 2 * TAPS + 2 * TAPS)

    @pl.when(step == steps - 1)
    def _():
        core = lax.axis_index("chan")
        half = n // 2
        for out_ref, first in ((mine_ref, core * half), (other_ref, (1 - core) * half)):
            for v in range(half):
                rows = pl.ds(first + v, lags, stride=n)
                value = acc0_ref[rows, :] + acc1_ref[rows, :]
                out_ref[:, v * lags : (v + 1) * lags] = value.T


def correlate(blocks, pieces):
    n = len(blocks)
    lags, width = blocks[0].shape
    k = PIECES * pieces[0].shape[1]
    steps = LE // (2 * TAPS)
    whole = pl.BlockSpec(memory_space=pltpu.VMEM)
    e_spec = pl.BlockSpec((2 * TAPS, k // PIECES, width), lambda i: (i, 0, 0))
    return pl.pallas_call(
        functools.partial(correlate_kernel, n, steps),
        grid=(steps,),
        in_specs=[whole] * n + [e_spec] * PIECES,
        out_specs=[whole, whole],
        out_shape=[jax.ShapeDtypeStruct((k, n * lags // 2), jnp.float32)] * 2,
        scratch_shapes=[
            pltpu.VMEM((n * lags, k), jnp.float32),
            pltpu.VMEM((n * lags, k), jnp.float32),
            pltpu.VMEM((width // LANES, (lags + LE + 2 * TAPS) * n, LANES), jnp.float32),
            pltpu.VMEM((width // LANES, (lags + LE) // GROUP, n, LANES), jnp.float32),
            pltpu.VMEM((width // LANES, lags * n, LANES), jnp.float32),
            pltpu.VMEM((n * lags, TAPS * width), jnp.bfloat16),
            pltpu.VMEM((n * lags, TAPS * width), jnp.bfloat16),
        ],
        compiler_params=pltpu.CompilerParams(vmem_limit_bytes=VMEM),
        cost_estimate=pl.CostEstimate(
            flops=2 * n * lags * LE * width * k,
            bytes_accessed=2 * LE * width * k,
            transcendentals=0,
        ),
    )(*blocks, *pieces)


def per_device(n, records, templates, offsets, masks):
    blocks, pieces = ring_gather(
        records.T, n, lambda piece: embed(templates, offsets, masks, piece)
    )
    mine, other = correlate(blocks, pieces)
    return mine + lax.ppermute(other, "chan", [(0, 1), (1, 0)])


def solution(mesh):
    return jax.shard_map(
        functools.partial(per_device, mesh.shape["blk"]),
        mesh=mesh,
        in_specs=(
            P("chan", ("groups", "blk")),
            P(None, ("groups", "blk"), "chan"),
            P(("groups", "blk"), "chan"),
            P(("groups", "blk"), "chan"),
        ),
        out_specs=P(("groups", "blk"), "chan"),
        check_vma=False,
    )
```

```python
import functools

import jax
import jax.numpy as jnp
from jax import lax
from jax.experimental import pallas as pl
from jax.experimental.pallas import tpu as pltpu
from jax.sharding import PartitionSpec as P

L = 100
LE = 104
SPAN = LE - L
EPS = 1e-06
LANES = 128
PIECES = 4
ROWS = 16
TAPS = 4
TILE = 512
GROUP = 8
VMEM = 56 * 1024 * 1024


def embed_kernel(t_ref, off_ref, mask_ref, e_ref):
    rows, cols = off_ref.shape
    for w in range(cols // LANES):
        lanes = slice(w * LANES, (w + 1) * LANES)
        total = jnp.zeros((rows, LANES), jnp.float32)
        for l in range(L):
            v = t_ref[l, :, lanes].astype(jnp.float32)
            total = total + v * v
        scale = lax.rsqrt(total / L + EPS) * mask_ref[:, lanes].astype(jnp.float32) / L
        off = off_ref[:, lanes]
        odd = ((off & 1) == 1).astype(jnp.bfloat16) > 0
        high = (off >= 2).astype(jnp.bfloat16) > 0
        full = (off == SPAN).astype(jnp.bfloat16) > 0
        zero = jnp.zeros((rows, LANES), jnp.bfloat16)
        plain = [zero] * SPAN
        moved = [zero] * 2
        for j in range(LE):
            sample = t_ref[j, :, lanes] if j < L else zero
            now = jnp.where(odd, plain[-1], sample)
            value = jnp.where(full, plain[0], jnp.where(high, moved[0], now))
            e_ref[j, :, lanes] = (value.astype(jnp.float32) * scale).astype(jnp.bfloat16)
            plain = plain[1:] + [sample]
            moved = moved[1:] + [now]


def embed(templates, offsets, masks, piece):
    k, channels = offsets.shape
    rows = k // PIECES
    steps = rows // ROWS
    first = piece * steps
    width = 2 * LANES
    return pl.pallas_call(
        embed_kernel,
        grid=(steps, channels // width),
        in_specs=[
            pl.BlockSpec((L, ROWS, width), lambda i, j: (0, first + i, j)),
            pl.BlockSpec((ROWS, width), lambda i, j: (first + i, j)),
            pl.BlockSpec((ROWS, width), lambda i, j: (first + i, j)),
        ],
        out_specs=pl.BlockSpec((LE, ROWS, width), lambda i, j: (0, i, j)),
        out_shape=jax.ShapeDtypeStruct((LE, rows, channels), jnp.bfloat16),
        compiler_params=pltpu.CompilerParams(vmem_limit_bytes=VMEM),
        cost_estimate=pl.CostEstimate(
            flops=20 * LE * rows * channels,
            bytes_accessed=2 * 2 * LE * rows * channels,
            transcendentals=0,
        ),
    )(templates, offsets, masks)


def ring_position(b, n):
    z, y = b // 2, b % 2
    return z * (1 - y) + (n - 1 - z) * y


def ring_block(p, n):
    half = n // 2
    low = (p < half) * 1 if isinstance(p, int) else (p < half).astype(jnp.int32)
    return low * (2 * p) + (1 - low) * (2 * (n - 1 - p) + 1)


def ring_gather(x, n, beside):
    order = [ring_block(p, n) for p in range(n)]
    up = [(order[p], order[(p + 1) % n]) for p in range(n)]
    down = [(order[(p + 1) % n], order[p]) for p in range(n)]
    blocks = {0: x}
    done = []
    a = b = x
    for step in range(1, n // 2 + 1):
        a = lax.ppermute(a, "blk", up)
        if step < n // 2:
            b = lax.ppermute(b, "blk", down)
        if step <= PIECES:
            done.append(beside(step - 1))
            a, b, done[-1] = lax.optimization_barrier((a, b, done[-1]))
        blocks[n - step] = a
        if step < n // 2:
            blocks[step] = b
    return [blocks[d] for d in range(n)], done


def prepare(n, block_refs, x_ref, g_ref, n_ref):
    lags, width = block_refs[0].shape
    me = ring_position(lax.axis_index("blk"), n)
    for d in range(n):
        v = ring_block(lax.rem(me + d, n), n)
        for w in range(width // LANES):
            for u in range(0, lags, 16):
                value = block_refs[d][u : u + 16, w * LANES : (w + 1) * LANES].astype(jnp.float32)
                for i in range(2):
                    x_ref[w, pl.ds((u + 8 * i) * n + v, 8, stride=n), :] = value[8 * i : 8 * i + 8]

        @pl.when(v > 0)
        def _():
            for w in range(width // LANES):
                for u in range(0, LE, 8):
                    value = x_ref[w, pl.ds(u * n + v, 8, stride=n), :]
                    x_ref[w, pl.ds((lags + u) * n + v - 1, 8, stride=n), :] = value

        @pl.when(v == 0)
        def _():
            for w in range(width // LANES):
                for u in range(0, LE, 8):
                    x_ref[w, pl.ds((lags + u) * n + n - 1, 8, stride=n), :] = jnp.zeros(
                        (8, LANES), jnp.float32
                    )

    x_ref[:, (lags + LE) * n :, :] = jnp.zeros((width // LANES, 2 * TAPS * n, LANES), jnp.float32)
    size = GROUP * n

    def energy(g, carry):
        for w in range(width // LANES):
            value = x_ref[w, pl.ds(pl.multiple_of(g * size, size), size), :].reshape(GROUP, n, LANES)
            g_ref[w, g] = jnp.sum(value * value, axis=0)
        return carry

    lax.fori_loop(0, (lags + LE) // GROUP, energy, 0)

    def norms(g, carry):
        for w in range(width // LANES):
            middle = g_ref[w, g + 1]
            for i in range(2, LE // GROUP):
                middle = middle + g_ref[w, g + i]
            left = x_ref[w, pl.ds(pl.multiple_of(g * size, size), size), :].reshape(GROUP, n, LANES)
            right = x_ref[w, pl.ds(pl.multiple_of(g * size + LE * n, size), size), :]
            right = right.reshape(GROUP, n, LANES)
            left = left * left
            right = right * right
            tails = [None] * GROUP
            tail = middle
            for r in range(GROUP - 1, -1, -1):
                tail = tail + left[r]
                tails[r] = tail
            head = None
            for r in range(GROUP):
                total = tails[r]
                if r > 0:
                    head = right[0] if r == 1 else head + right[r - 1]
                    total = total + head
                row = pl.ds(pl.multiple_of((g * GROUP + r) * n, n), n)
                n_ref[w, row, :] = lax.rsqrt(total / LE + EPS)
        return carry

    lax.fori_loop(0, lags // GROUP, norms, 0)


def build(x_ref, n_ref, w_ref, n, tap0, m):
    tiles = x_ref.shape[0]
    size = 8 * n
    for i in range(TILE // size):
        row = m * TILE + i * size
        rows = pl.ds(pl.multiple_of(row, size), size)
        for w in range(tiles):
            norm = n_ref[w, rows, :]
            xs = x_ref[w, pl.ds(pl.multiple_of(row + tap0 * n, n), (TAPS + 7) * n), :]
            for tap in range(TAPS):
                value = (xs[tap * n : tap * n + size] * norm).astype(jnp.bfloat16)
                w_ref[rows, (tap * tiles + w) * LANES : (tap * tiles + w + 1) * LANES] = value


def correlate_kernel(n, steps, *refs):
    blocks = refs[:n]
    e_refs = refs[n : n + PIECES]
    mine_ref, other_ref, acc_ref, turned_ref, x_ref, g_ref, n_ref, even_ref, odd_ref = refs[n + PIECES :]
    lags, width = blocks[0].shape
    tiles = n * lags // TILE
    step = pl.program_id(0)

    @pl.when(step == 0)
    def _():
        prepare(n, blocks, x_ref, g_ref, n_ref)
        acc_ref[...] = jnp.zeros_like(acc_ref)

        def first(m, carry):
            build(x_ref, n_ref, even_ref, n, 0, m)
            return carry

        lax.fori_loop(0, tiles, first, 0)

    def advance(now_ref, later_ref, part, tap0):
        weights = jnp.concatenate(
            [
                jnp.concatenate([e_ref[part * TAPS + tap] for e_ref in e_refs], axis=0)
                for tap in range(TAPS)
            ],
            axis=1,
        )

        def tile(m, carry):
            rows = pl.ds(pl.multiple_of(m * TILE, TILE), TILE)
            acc_ref[:, rows] += lax.dot_general(
                weights,
                now_ref[rows, :],
                (((1,), (1,)), ((), ())),
                preferred_element_type=jnp.float32,
            )
            build(x_ref, n_ref, later_ref, n, tap0, m)
            return carry

        lax.fori_loop(0, tiles, tile, 0)

    advance(even_ref, odd_ref, 0, step * 2 * TAPS + TAPS)
    advance(odd_ref, even_ref, 1, step * 2 * TAPS + 2 * TAPS)

    @pl.when(step == steps - 1)
    def _():
        for u in range(0, n * lags, LANES):
            turned_ref[u : u + LANES, :] = acc_ref[:, u : u + LANES].T
        core = lax.axis_index("chan")
        half = n // 2
        for out_ref, first in ((mine_ref, core * half), (other_ref, (1 - core) * half)):
            for v in range(half):
                value = turned_ref[pl.ds(first + v, lags, stride=n), :]
                out_ref[:, v * lags : (v + 1) * lags] = value.T


def correlate(blocks, pieces):
    n = len(blocks)
    lags, width = blocks[0].shape
    k = PIECES * pieces[0].shape[1]
    steps = LE // (2 * TAPS)
    whole = pl.BlockSpec(memory_space=pltpu.VMEM)
    e_spec = pl.BlockSpec((2 * TAPS, k // PIECES, width), lambda i: (i, 0, 0))
    return pl.pallas_call(
        functools.partial(correlate_kernel, n, steps),
        grid=(steps,),
        in_specs=[whole] * n + [e_spec] * PIECES,
        out_specs=[whole, whole],
        out_shape=[jax.ShapeDtypeStruct((k, n * lags // 2), jnp.float32)] * 2,
        scratch_shapes=[
            pltpu.VMEM((k, n * lags), jnp.float32),
            pltpu.VMEM((n * lags, k), jnp.float32),
            pltpu.VMEM((width // LANES, (lags + LE + 2 * TAPS) * n, LANES), jnp.float32),
            pltpu.VMEM((width // LANES, (lags + LE) // GROUP, n, LANES), jnp.float32),
            pltpu.VMEM((width // LANES, lags * n, LANES), jnp.float32),
            pltpu.VMEM((n * lags, TAPS * width), jnp.bfloat16),
            pltpu.VMEM((n * lags, TAPS * width), jnp.bfloat16),
        ],
        compiler_params=pltpu.CompilerParams(vmem_limit_bytes=VMEM),
        cost_estimate=pl.CostEstimate(
            flops=2 * n * lags * LE * width * k,
            bytes_accessed=2 * LE * width * k,
            transcendentals=0,
        ),
    )(*blocks, *pieces)


def per_device(n, records, templates, offsets, masks):
    blocks, pieces = ring_gather(
        records.T, n, lambda piece: embed(templates, offsets, masks, piece)
    )
    mine, other = correlate(blocks, pieces)
    return mine + lax.ppermute(other, "chan", [(0, 1), (1, 0)])


def solution(mesh):
    return jax.shard_map(
        functools.partial(per_device, mesh.shape["blk"]),
        mesh=mesh,
        in_specs=(
            P("chan", ("groups", "blk")),
            P(None, ("groups", "blk"), "chan"),
            P(("groups", "blk"), "chan"),
            P(("groups", "blk"), "chan"),
        ),
        out_specs=P(("groups", "blk"), "chan"),
        check_vma=False,
    )
```

```python
import functools

import jax
import jax.numpy as jnp
from jax import lax
from jax.experimental import pallas as pl
from jax.experimental.pallas import tpu as pltpu
from jax.sharding import PartitionSpec as P

L = 100
LE = 104
SPAN = LE - L
EPS = 1e-06
LANES = 128
PIECES = 4
ROWS = 16
TAPS = 4
TILE = 512
GROUP = 8
VMEM = 56 * 1024 * 1024


def embed_kernel(t_ref, off_ref, mask_ref, e_ref):
    rows, cols = off_ref.shape
    for w in range(cols // LANES):
        lanes = slice(w * LANES, (w + 1) * LANES)
        total = jnp.zeros((rows, LANES), jnp.float32)
        for l in range(L):
            v = t_ref[l, :, lanes].astype(jnp.float32)
            total = total + v * v
        scale = lax.rsqrt(total / L + EPS) * mask_ref[:, lanes].astype(jnp.float32) / L
        off = off_ref[:, lanes]
        odd = ((off & 1) == 1).astype(jnp.bfloat16) > 0
        high = (off >= 2).astype(jnp.bfloat16) > 0
        full = (off == SPAN).astype(jnp.bfloat16) > 0
        zero = jnp.zeros((rows, LANES), jnp.bfloat16)
        plain = [zero] * SPAN
        moved = [zero] * 2
        for j in range(LE):
            sample = t_ref[j, :, lanes] if j < L else zero
            now = jnp.where(odd, plain[-1], sample)
            value = jnp.where(full, plain[0], jnp.where(high, moved[0], now))
            e_ref[j, :, lanes] = (value.astype(jnp.float32) * scale).astype(jnp.bfloat16)
            plain = plain[1:] + [sample]
            moved = moved[1:] + [now]


def embed(templates, offsets, masks, piece):
    k, channels = offsets.shape
    rows = k // PIECES
    steps = rows // ROWS
    first = piece * steps
    width = 2 * LANES
    return pl.pallas_call(
        embed_kernel,
        grid=(steps, channels // width),
        in_specs=[
            pl.BlockSpec((L, ROWS, width), lambda i, j: (0, first + i, j)),
            pl.BlockSpec((ROWS, width), lambda i, j: (first + i, j)),
            pl.BlockSpec((ROWS, width), lambda i, j: (first + i, j)),
        ],
        out_specs=pl.BlockSpec((LE, ROWS, width), lambda i, j: (0, i, j)),
        out_shape=jax.ShapeDtypeStruct((LE, rows, channels), jnp.bfloat16),
        compiler_params=pltpu.CompilerParams(vmem_limit_bytes=VMEM),
        cost_estimate=pl.CostEstimate(
            flops=20 * LE * rows * channels,
            bytes_accessed=2 * 2 * LE * rows * channels,
            transcendentals=0,
        ),
    )(templates, offsets, masks)


def ring_position(b, n):
    z, y = b // 2, b % 2
    return z * (1 - y) + (n - 1 - z) * y


def ring_block(p, n):
    half = n // 2
    low = (p < half) * 1 if isinstance(p, int) else (p < half).astype(jnp.int32)
    return low * (2 * p) + (1 - low) * (2 * (n - 1 - p) + 1)


def ring_gather(x, n, beside):
    order = [ring_block(p, n) for p in range(n)]
    up = [(order[p], order[(p + 1) % n]) for p in range(n)]
    down = [(order[(p + 1) % n], order[p]) for p in range(n)]
    blocks = {0: x}
    done = []
    a = b = x
    for step in range(1, n // 2 + 1):
        a = lax.ppermute(a, "blk", up)
        if step < n // 2:
            b = lax.ppermute(b, "blk", down)
        if step <= PIECES:
            done.append(beside(step - 1))
            a, b, done[-1] = lax.optimization_barrier((a, b, done[-1]))
        blocks[n - step] = a
        if step < n // 2:
            blocks[step] = b
    return [blocks[d] for d in range(n)], done


def shift(value, lanes):
    moved = pltpu.roll(value, LANES - lanes, 1)
    lane = lax.broadcasted_iota(jnp.int32, value.shape, 1)
    return jnp.where(lane < LANES - lanes, moved, 0.0)


def extend(x_ref, first, period, start, size):
    rows = pl.ds(start, size)
    for i in range(TAPS):
        before = x_ref[first + i - period, rows, :].astype(jnp.float32)
        x_ref[first + i, rows, :] = shift(before, 1).astype(jnp.bfloat16)


def prepare(n, block_refs, flat_ref, x_ref, n_ref):
    lags, width = block_refs[0].shape
    period = n * lags // LANES
    me = ring_position(lax.axis_index("blk"), n)
    for d in range(n):
        where = ring_block(lax.rem(me + d, n), n)
        for w in range(width // LANES):
            flat_ref[w, pl.ds(pl.multiple_of(where * lags, lags), lags), :] = block_refs[d][
                :, w * LANES : (w + 1) * LANES
            ].astype(jnp.float32)

    def turn(u, carry):
        for w in range(width // LANES):
            value = flat_ref[w, pl.ds(u, LANES, stride=period), :]
            x_ref[u, w * LANES : (w + 1) * LANES, :] = value.T.astype(jnp.bfloat16)
        return carry

    lax.fori_loop(0, period, turn, 0)

    groups = period // GROUP

    def norms(i, carry):
        rows = pl.ds(pl.multiple_of(i * 16, 16), 16)
        square = []
        for u in range(period):
            value = x_ref[u, rows, :].astype(jnp.float32)
            square.append(value * value)
        sums = []
        for g in range(groups + LE // GROUP - 1):
            if g < groups:
                total = square[g * GROUP]
                for r in range(1, GROUP):
                    total = total + square[g * GROUP + r]
            else:
                total = shift(sums[g - groups], 1)
            sums.append(total)
        for g in range(groups):
            tail = sums[g + 1]
            for j in range(2, LE // GROUP):
                tail = tail + sums[g + j]
            tails = [None] * GROUP
            for r in range(GROUP - 1, -1, -1):
                tail = tail + square[g * GROUP + r]
                tails[r] = tail
            head = None
            for r in range(GROUP):
                total = tails[r]
                if r > 0:
                    s = g * GROUP + LE + r - 1
                    value = shift(square[s % period], s // period)
                    head = value if r == 1 else head + value
                    total = total + head
                n_ref[g * GROUP + r, rows, :] = lax.rsqrt(total / LE + EPS)
        return carry

    lax.fori_loop(0, width // 16, norms, 0)


def build(x_ref, n_ref, w_ref, tap0, start, size):
    period, width, _ = n_ref.shape
    for i in range(size // 16):
        first = pl.multiple_of(start + i * 16, 16)
        rows = pl.ds(first, 16)
        for u0 in range(0, period, 8):
            norm = [n_ref[u0 + u, rows, :] for u in range(8)]
            for s in range(TAPS + 7):
                value = x_ref[tap0 + u0 + s, rows, :].astype(jnp.float32)
                for tap in range(max(0, s - 7), min(TAPS, s + 1)):
                    u = s - tap
                    where = pl.ds(pl.multiple_of(tap * width + first, 16), 16)
                    lanes = slice((u0 + u) * LANES, (u0 + u + 1) * LANES)
                    w_ref[where, lanes] = (value * norm[u]).astype(jnp.bfloat16)


def correlate_kernel(n, steps, *refs):
    blocks = refs[:n]
    e_refs = refs[n : n + PIECES]
    mine_ref, other_ref, acc_ref, turned_ref, flat_ref, x_ref, n_ref, even_ref, odd_ref = refs[
        n + PIECES :
    ]
    lags, width = blocks[0].shape
    period = n_ref.shape[0]
    tiles = n * lags // TILE
    share = width // tiles
    step = pl.program_id(0)

    @pl.when(step == 0)
    def _():
        prepare(n, blocks, flat_ref, x_ref, n_ref)
        acc_ref[...] = jnp.zeros_like(acc_ref)

        def first(i, carry):
            start = pl.multiple_of(i * 16, 16)
            extend(x_ref, period, period, start, 16)
            extend(x_ref, period + TAPS, period, start, 16)
            build(x_ref, n_ref, even_ref, 0, start, 16)
            return carry

        lax.fori_loop(0, width // 16, first, 0)

    def advance(now_ref, later_ref, part, tap0):
        def tile(m, carry):
            columns = pl.ds(pl.multiple_of(m * TILE, TILE), TILE)
            weights = jnp.concatenate(
                [
                    jnp.concatenate([e_ref[part * TAPS + tap] for e_ref in e_refs], axis=0)
                    for tap in range(TAPS)
                ],
                axis=1,
            )
            acc_ref[:, columns] += jnp.dot(
                weights, now_ref[:, columns], preferred_element_type=jnp.float32
            )
            start = pl.multiple_of(m * share, share)
            build(x_ref, n_ref, later_ref, tap0, start, share)
            extend(x_ref, tap0 + TAPS + period, period, start, share)
            return carry

        lax.fori_loop(0, tiles, tile, 0)

    advance(even_ref, odd_ref, 0, step * 2 * TAPS + TAPS)
    advance(odd_ref, even_ref, 1, step * 2 * TAPS + 2 * TAPS)

    @pl.when(step == steps - 1)
    def _():
        for u in range(period):
            value = acc_ref[:, u * LANES : (u + 1) * LANES]
            turned_ref[pl.ds(u, LANES, stride=period), :] = value.T
        core = lax.axis_index("chan")
        half = n * lags // 2
        for out_ref, first in ((mine_ref, core * half), (other_ref, (1 - core) * half)):
            for v in range(0, half, LANES):
                rows = pl.ds(pl.multiple_of(first + v, LANES), LANES)
                out_ref[:, v : v + LANES] = turned_ref[rows, :].T


def correlate(blocks, pieces):
    n = len(blocks)
    lags, width = blocks[0].shape
    k = PIECES * pieces[0].shape[1]
    period = n * lags // LANES
    steps = LE // (2 * TAPS)
    whole = pl.BlockSpec(memory_space=pltpu.VMEM)
    e_spec = pl.BlockSpec((2 * TAPS, k // PIECES, width), lambda i: (i, 0, 0))
    return pl.pallas_call(
        functools.partial(correlate_kernel, n, steps),
        grid=(steps,),
        in_specs=[whole] * n + [e_spec] * PIECES,
        out_specs=[whole, whole],
        out_shape=[jax.ShapeDtypeStruct((k, n * lags // 2), jnp.float32)] * 2,
        scratch_shapes=[
            pltpu.VMEM((k, n * lags), jnp.float32),
            pltpu.VMEM((n * lags, k), jnp.float32),
            pltpu.VMEM((width // LANES, n * lags, LANES), jnp.float32),
            pltpu.VMEM((period + LE + 2 * TAPS, width, LANES), jnp.bfloat16),
            pltpu.VMEM((period, width, LANES), jnp.float32),
            pltpu.VMEM((TAPS * width, n * lags), jnp.bfloat16),
            pltpu.VMEM((TAPS * width, n * lags), jnp.bfloat16),
        ],
        compiler_params=pltpu.CompilerParams(vmem_limit_bytes=VMEM),
        cost_estimate=pl.CostEstimate(
            flops=2 * n * lags * LE * width * k,
            bytes_accessed=2 * LE * width * k,
            transcendentals=0,
        ),
    )(*blocks, *pieces)


def per_device(n, records, templates, offsets, masks):
    blocks, pieces = ring_gather(
        records.T, n, lambda piece: embed(templates, offsets, masks, piece)
    )
    mine, other = correlate(blocks, pieces)
    return mine + lax.ppermute(other, "chan", [(0, 1), (1, 0)])


def solution(mesh):
    return jax.shard_map(
        functools.partial(per_device, mesh.shape["blk"]),
        mesh=mesh,
        in_specs=(
            P("chan", ("groups", "blk")),
            P(None, ("groups", "blk"), "chan"),
            P(("groups", "blk"), "chan"),
            P(("groups", "blk"), "chan"),
        ),
        out_specs=P(("groups", "blk"), "chan"),
        check_vma=False,
    )
```

```python
import functools

import jax
import jax.numpy as jnp
from jax import lax
from jax.experimental import pallas as pl
from jax.experimental.pallas import tpu as pltpu
from jax.sharding import PartitionSpec as P

L = 100
LE = 104
SPAN = LE - L
EPS = 1e-06
LANES = 128
PIECES = 4
ROWS = 16
TAPS = 4
TILE = 512
GROUP = 8
VMEM = 56 * 1024 * 1024


def embed_kernel(t_ref, off_ref, mask_ref, e_ref):
    rows, cols = off_ref.shape
    for w in range(cols // LANES):
        lanes = slice(w * LANES, (w + 1) * LANES)
        total = jnp.zeros((rows, LANES), jnp.float32)
        for l in range(L):
            v = t_ref[l, :, lanes].astype(jnp.float32)
            total = total + v * v
        scale = lax.rsqrt(total / L + EPS) * mask_ref[:, lanes].astype(jnp.float32) / L
        off = off_ref[:, lanes]
        odd = ((off & 1) == 1).astype(jnp.bfloat16) > 0
        high = (off >= 2).astype(jnp.bfloat16) > 0
        full = (off == SPAN).astype(jnp.bfloat16) > 0
        zero = jnp.zeros((rows, LANES), jnp.bfloat16)
        plain = [zero] * SPAN
        moved = [zero] * 2
        for j in range(LE):
            sample = t_ref[j, :, lanes] if j < L else zero
            now = jnp.where(odd, plain[-1], sample)
            value = jnp.where(full, plain[0], jnp.where(high, moved[0], now))
            e_ref[j, :, lanes] = (value.astype(jnp.float32) * scale).astype(jnp.bfloat16)
            plain = plain[1:] + [sample]
            moved = moved[1:] + [now]


def embed(templates, offsets, masks, piece):
    k, channels = offsets.shape
    rows = k // PIECES
    steps = rows // ROWS
    first = piece * steps
    width = 2 * LANES
    return pl.pallas_call(
        embed_kernel,
        grid=(steps, channels // width),
        in_specs=[
            pl.BlockSpec((L, ROWS, width), lambda i, j: (0, first + i, j)),
            pl.BlockSpec((ROWS, width), lambda i, j: (first + i, j)),
            pl.BlockSpec((ROWS, width), lambda i, j: (first + i, j)),
        ],
        out_specs=pl.BlockSpec((LE, ROWS, width), lambda i, j: (0, i, j)),
        out_shape=jax.ShapeDtypeStruct((LE, rows, channels), jnp.bfloat16),
        compiler_params=pltpu.CompilerParams(vmem_limit_bytes=VMEM),
        cost_estimate=pl.CostEstimate(
            flops=20 * LE * rows * channels,
            bytes_accessed=2 * 2 * LE * rows * channels,
            transcendentals=0,
        ),
    )(templates, offsets, masks)


def ring_position(b, n):
    z, y = b // 2, b % 2
    return z * (1 - y) + (n - 1 - z) * y


def ring_block(p, n):
    half = n // 2
    low = (p < half) * 1 if isinstance(p, int) else (p < half).astype(jnp.int32)
    return low * (2 * p) + (1 - low) * (2 * (n - 1 - p) + 1)


def ring_gather(x, n, beside):
    order = [ring_block(p, n) for p in range(n)]
    up = [(order[p], order[(p + 1) % n]) for p in range(n)]
    down = [(order[(p + 1) % n], order[p]) for p in range(n)]
    blocks = {0: x}
    done = []
    a = b = x
    for step in range(1, n // 2 + 1):
        a = lax.ppermute(a, "blk", up)
        if step < n // 2:
            b = lax.ppermute(b, "blk", down)
        if step <= PIECES:
            done.append(beside(step - 1))
            a, b, done[-1] = lax.optimization_barrier((a, b, done[-1]))
        blocks[n - step] = a
        if step < n // 2:
            blocks[step] = b
    return [blocks[d] for d in range(n)], done


def shift(value, lanes):
    moved = pltpu.roll(value, LANES - lanes, 1)
    lane = lax.broadcasted_iota(jnp.int32, value.shape, 1)
    return jnp.where(lane < LANES - lanes, moved, 0.0)


def extend(x_ref, first, period, start, size):
    rows = pl.ds(start, size)
    for i in range(TAPS):
        before = x_ref[first + i - period, rows, :].astype(jnp.float32)
        x_ref[first + i, rows, :] = shift(before, 1).astype(jnp.bfloat16)


def prepare(n, block_refs, flat_ref, x_ref, high_ref, low_ref):
    lags, width = block_refs[0].shape
    period = n * lags // LANES
    me = ring_position(lax.axis_index("blk"), n)
    for d in range(n):
        where = ring_block(lax.rem(me + d, n), n)
        for w in range(width // LANES):
            flat_ref[w, pl.ds(pl.multiple_of(where * lags, lags), lags), :] = block_refs[d][
                :, w * LANES : (w + 1) * LANES
            ].astype(jnp.float32)

    def turn(u, carry):
        for w in range(width // LANES):
            value = flat_ref[w, pl.ds(u, LANES, stride=period), :]
            x_ref[u, w * LANES : (w + 1) * LANES, :] = value.T.astype(jnp.bfloat16)
        return carry

    lax.fori_loop(0, period, turn, 0)

    groups = period // GROUP

    def norms(i, carry):
        rows = pl.ds(pl.multiple_of(i * 16, 16), 16)
        square = []
        for u in range(period):
            value = x_ref[u, rows, :].astype(jnp.float32)
            square.append(value * value)
        sums = []
        for g in range(groups + LE // GROUP - 1):
            if g < groups:
                total = square[g * GROUP]
                for r in range(1, GROUP):
                    total = total + square[g * GROUP + r]
            else:
                total = shift(sums[g - groups], 1)
            sums.append(total)
        for g in range(groups):
            tail = sums[g + 1]
            for j in range(2, LE // GROUP):
                tail = tail + sums[g + j]
            tails = [None] * GROUP
            for r in range(GROUP - 1, -1, -1):
                tail = tail + square[g * GROUP + r]
                tails[r] = tail
            head = None
            for r in range(GROUP):
                total = tails[r]
                if r > 0:
                    s = g * GROUP + LE + r - 1
                    value = shift(square[s % period], s // period)
                    head = value if r == 1 else head + value
                    total = total + head
                norm = lax.rsqrt(total / LE + EPS)
                high = norm.astype(jnp.bfloat16)
                high_ref[g * GROUP + r, rows, :] = high
                low_ref[g * GROUP + r, rows, :] = (norm - high.astype(jnp.float32)).astype(
                    jnp.bfloat16
                )
        return carry

    lax.fori_loop(0, width // 16, norms, 0)


def build(x_ref, high_ref, low_ref, w_ref, tap0, start, size):
    period, width, _ = high_ref.shape
    for i in range(size // 16):
        first = pl.multiple_of(start + i * 16, 16)
        rows = pl.ds(first, 16)
        for u0 in range(0, period, 8):
            high = [high_ref[u0 + u, rows, :] for u in range(8)]
            low = [low_ref[u0 + u, rows, :] for u in range(8)]
            for s in range(TAPS + 7):
                value = x_ref[tap0 + u0 + s, rows, :]
                for tap in range(max(0, s - 7), min(TAPS, s + 1)):
                    u = s - tap
                    where = pl.ds(pl.multiple_of(tap * width + first, 16), 16)
                    lanes = slice((u0 + u) * LANES, (u0 + u + 1) * LANES)
                    w_ref[where, lanes] = value * high[u] + value * low[u]


def correlate_kernel(n, steps, *refs):
    blocks = refs[:n]
    e_refs = refs[n : n + PIECES]
    mine_ref, other_ref, acc_ref, turned_ref, flat_ref, x_ref, high_ref, low_ref, even_ref, odd_ref = refs[
        n + PIECES :
    ]
    lags, width = blocks[0].shape
    period = high_ref.shape[0]
    tiles = n * lags // TILE
    share = width // tiles
    step = pl.program_id(0)

    @pl.when(step == 0)
    def _():
        prepare(n, blocks, flat_ref, x_ref, high_ref, low_ref)
        acc_ref[...] = jnp.zeros_like(acc_ref)

        def first(i, carry):
            start = pl.multiple_of(i * 16, 16)
            extend(x_ref, period, period, start, 16)
            extend(x_ref, period + TAPS, period, start, 16)
            build(x_ref, high_ref, low_ref, even_ref, 0, start, 16)
            return carry

        lax.fori_loop(0, width // 16, first, 0)

    def advance(now_ref, later_ref, part, tap0):
        def tile(m, carry):
            columns = pl.ds(pl.multiple_of(m * TILE, TILE), TILE)
            weights = jnp.concatenate(
                [
                    jnp.concatenate([e_ref[part * TAPS + tap] for e_ref in e_refs], axis=0)
                    for tap in range(TAPS)
                ],
                axis=1,
            )
            acc_ref[:, columns] += jnp.dot(
                weights, now_ref[:, columns], preferred_element_type=jnp.float32
            )
            start = pl.multiple_of(m * share, share)
            build(x_ref, high_ref, low_ref, later_ref, tap0, start, share)
            extend(x_ref, tap0 + TAPS + period, period, start, share)
            return carry

        lax.fori_loop(0, tiles, tile, 0)

    advance(even_ref, odd_ref, 0, step * 2 * TAPS + TAPS)
    advance(odd_ref, even_ref, 1, step * 2 * TAPS + 2 * TAPS)

    @pl.when(step == steps - 1)
    def _():
        for u in range(period):
            value = acc_ref[:, u * LANES : (u + 1) * LANES]
            turned_ref[pl.ds(u, LANES, stride=period), :] = value.T
        core = lax.axis_index("chan")
        half = n * lags // 2
        for out_ref, first in ((mine_ref, core * half), (other_ref, (1 - core) * half)):
            for v in range(0, half, LANES):
                rows = pl.ds(pl.multiple_of(first + v, LANES), LANES)
                out_ref[:, v : v + LANES] = turned_ref[rows, :].T


def correlate(blocks, pieces):
    n = len(blocks)
    lags, width = blocks[0].shape
    k = PIECES * pieces[0].shape[1]
    period = n * lags // LANES
    steps = LE // (2 * TAPS)
    whole = pl.BlockSpec(memory_space=pltpu.VMEM)
    e_spec = pl.BlockSpec((2 * TAPS, k // PIECES, width), lambda i: (i, 0, 0))
    return pl.pallas_call(
        functools.partial(correlate_kernel, n, steps),
        grid=(steps,),
        in_specs=[whole] * n + [e_spec] * PIECES,
        out_specs=[whole, whole],
        out_shape=[jax.ShapeDtypeStruct((k, n * lags // 2), jnp.float32)] * 2,
        scratch_shapes=[
            pltpu.VMEM((k, n * lags), jnp.float32),
            pltpu.VMEM((n * lags, k), jnp.float32),
            pltpu.VMEM((width // LANES, n * lags, LANES), jnp.float32),
            pltpu.VMEM((period + LE + 2 * TAPS, width, LANES), jnp.bfloat16),
            pltpu.VMEM((period, width, LANES), jnp.bfloat16),
            pltpu.VMEM((period, width, LANES), jnp.bfloat16),
            pltpu.VMEM((TAPS * width, n * lags), jnp.bfloat16),
            pltpu.VMEM((TAPS * width, n * lags), jnp.bfloat16),
        ],
        compiler_params=pltpu.CompilerParams(vmem_limit_bytes=VMEM),
        cost_estimate=pl.CostEstimate(
            flops=2 * n * lags * LE * width * k,
            bytes_accessed=2 * LE * width * k,
            transcendentals=0,
        ),
    )(*blocks, *pieces)


def per_device(n, records, templates, offsets, masks):
    blocks, pieces = ring_gather(
        records.T, n, lambda piece: embed(templates, offsets, masks, piece)
    )
    mine, other = correlate(blocks, pieces)
    return mine + lax.ppermute(other, "chan", [(0, 1), (1, 0)])


def solution(mesh):
    return jax.shard_map(
        functools.partial(per_device, mesh.shape["blk"]),
        mesh=mesh,
        in_specs=(
            P("chan", ("groups", "blk")),
            P(None, ("groups", "blk"), "chan"),
            P(("groups", "blk"), "chan"),
            P(("groups", "blk"), "chan"),
        ),
        out_specs=P(("groups", "blk"), "chan"),
        check_vma=False,
    )
```

```python
import functools

import jax
import jax.numpy as jnp
from jax import lax
from jax.experimental import pallas as pl
from jax.experimental.pallas import tpu as pltpu
from jax.sharding import PartitionSpec as P

L = 100
LE = 104
SPAN = LE - L
EPS = 1e-06
LANES = 128
PIECES = 4
ROWS = 16
TAPS = 8
TILE = 256
GROUP = 8
EMBED_VMEM = 8 * 1024 * 1024
VMEM = 28 * 1024 * 1024


def embed_kernel(t_ref, off_ref, mask_ref, e_ref):
    rows, cols = off_ref.shape
    for w in range(cols // LANES):
        lanes = slice(w * LANES, (w + 1) * LANES)
        total = jnp.zeros((rows, LANES), jnp.float32)
        for l in range(L):
            v = t_ref[l, :, lanes].astype(jnp.float32)
            total = total + v * v
        scale = lax.rsqrt(total / L + EPS) * mask_ref[:, lanes].astype(jnp.float32) / L
        off = off_ref[:, lanes]
        odd = ((off & 1) == 1).astype(jnp.bfloat16) > 0
        high = (off >= 2).astype(jnp.bfloat16) > 0
        full = (off == SPAN).astype(jnp.bfloat16) > 0
        zero = jnp.zeros((rows, LANES), jnp.bfloat16)
        plain = [zero] * SPAN
        moved = [zero] * 2
        for j in range(LE):
            sample = t_ref[j, :, lanes] if j < L else zero
            now = jnp.where(odd, plain[-1], sample)
            value = jnp.where(full, plain[0], jnp.where(high, moved[0], now))
            e_ref[j, :, lanes] = (value.astype(jnp.float32) * scale).astype(jnp.bfloat16)
            plain = plain[1:] + [sample]
            moved = moved[1:] + [now]


def embed(templates, offsets, masks, piece):
    k, channels = offsets.shape
    rows = k // PIECES
    steps = rows // ROWS
    first = piece * steps
    width = 2 * LANES
    return pl.pallas_call(
        embed_kernel,
        grid=(steps, channels // width),
        in_specs=[
            pl.BlockSpec((L, ROWS, width), lambda i, j: (0, first + i, j)),
            pl.BlockSpec((ROWS, width), lambda i, j: (first + i, j)),
            pl.BlockSpec((ROWS, width), lambda i, j: (first + i, j)),
        ],
        out_specs=pl.BlockSpec((LE, ROWS, width), lambda i, j: (0, i, j)),
        out_shape=jax.ShapeDtypeStruct((LE, rows, channels), jnp.bfloat16),
        compiler_params=pltpu.CompilerParams(vmem_limit_bytes=EMBED_VMEM),
        cost_estimate=pl.CostEstimate(
            flops=20 * LE * rows * channels,
            bytes_accessed=2 * 2 * LE * rows * channels,
            transcendentals=0,
        ),
    )(templates, offsets, masks)


def ring_position(b, n):
    z, y = b // 2, b % 2
    return z * (1 - y) + (n - 1 - z) * y


def ring_block(p, n):
    half = n // 2
    low = (p < half) * 1 if isinstance(p, int) else (p < half).astype(jnp.int32)
    return low * (2 * p) + (1 - low) * (2 * (n - 1 - p) + 1)


def ring_gather(x, n, beside):
    order = [ring_block(p, n) for p in range(n)]
    up = [(order[p], order[(p + 1) % n]) for p in range(n)]
    down = [(order[(p + 1) % n], order[p]) for p in range(n)]
    blocks = {0: x}
    done = []
    a = b = x
    for step in range(1, n // 2 + 1):
        a = lax.ppermute(a, "blk", up)
        if step < n // 2:
            b = lax.ppermute(b, "blk", down)
        if step <= PIECES:
            done.append(beside(step - 1))
            a, b, done[-1] = lax.optimization_barrier((a, b, done[-1]))
        blocks[n - step] = a
        if step < n // 2:
            blocks[step] = b
    return [blocks[d] for d in range(n)], done


def prepare(n, block_refs, x_ref, g_ref, n_ref):
    lags, width = block_refs[0].shape
    me = ring_position(lax.axis_index("blk"), n)
    for d in range(n):
        v = ring_block(lax.rem(me + d, n), n)
        for w in range(width // LANES):
            for u in range(0, lags, 16):
                value = block_refs[d][u : u + 16, w * LANES : (w + 1) * LANES].astype(jnp.float32)
                for i in range(2):
                    x_ref[w, pl.ds((u + 8 * i) * n + v, 8, stride=n), :] = value[8 * i : 8 * i + 8]

        @pl.when(v > 0)
        def _():
            for w in range(width // LANES):
                for u in range(0, LE, 8):
                    value = x_ref[w, pl.ds(u * n + v, 8, stride=n), :]
                    x_ref[w, pl.ds((lags + u) * n + v - 1, 8, stride=n), :] = value

        @pl.when(v == 0)
        def _():
            for w in range(width // LANES):
                for u in range(0, LE, 8):
                    x_ref[w, pl.ds((lags + u) * n + n - 1, 8, stride=n), :] = jnp.zeros(
                        (8, LANES), jnp.float32
                    )

    size = GROUP * n

    def energy(g, carry):
        for w in range(width // LANES):
            value = x_ref[w, pl.ds(pl.multiple_of(g * size, size), size), :].reshape(GROUP, n, LANES)
            g_ref[w, g] = jnp.sum(value * value, axis=0)
        return carry

    lax.fori_loop(0, (lags + LE) // GROUP, energy, 0)

    def norms(g, carry):
        for w in range(width // LANES):
            middle = g_ref[w, g + 1]
            for i in range(2, LE // GROUP):
                middle = middle + g_ref[w, g + i]
            left = x_ref[w, pl.ds(pl.multiple_of(g * size, size), size), :].reshape(GROUP, n, LANES)
            right = x_ref[w, pl.ds(pl.multiple_of(g * size + LE * n, size), size), :]
            right = right.reshape(GROUP, n, LANES)
            left = left * left
            right = right * right
            tails = [None] * GROUP
            tail = middle
            for r in range(GROUP - 1, -1, -1):
                tail = tail + left[r]
                tails[r] = tail
            head = None
            for r in range(GROUP):
                total = tails[r]
                if r > 0:
                    head = right[0] if r == 1 else head + right[r - 1]
                    total = total + head
                row = pl.ds(pl.multiple_of((g * GROUP + r) * n, n), n)
                n_ref[w, row, :] = lax.rsqrt(total / LE + EPS)
        return carry

    lax.fori_loop(0, lags // GROUP, norms, 0)


def correlate_kernel(n, steps, *refs):
    blocks = refs[:n]
    e_refs = refs[n : n + PIECES]
    mine_ref, other_ref, acc_ref, x_ref, g_ref, n_ref = refs[n + PIECES :]
    lags, width = blocks[0].shape
    step = pl.program_id(0)

    @pl.when(step == 0)
    def _():
        prepare(n, blocks, x_ref, g_ref, n_ref)
        acc_ref[...] = jnp.zeros_like(acc_ref)

    def tile(m, carry):
        rows = pl.ds(pl.multiple_of(m * TILE, TILE), TILE)
        parts = []
        for tap in range(TAPS):
            first = pl.multiple_of(m * TILE + (step * TAPS + tap) * n, n)
            for w in range(width // LANES):
                value = x_ref[w, pl.ds(first, TILE), :] * n_ref[w, rows, :]
                parts.append(value.astype(jnp.bfloat16))
        windows = jnp.concatenate(parts, axis=1)
        weights = jnp.concatenate(
            [jnp.concatenate([e_ref[tap] for e_ref in e_refs], axis=0) for tap in range(TAPS)],
            axis=1,
        )
        acc_ref[rows, :] += lax.dot_general(
            windows, weights, (((1,), (1,)), ((), ())), preferred_element_type=jnp.float32
        )
        return carry

    lax.fori_loop(0, n * lags // TILE, tile, 0)

    @pl.when(step == steps - 1)
    def _():
        core = lax.axis_index("chan")
        half = n // 2
        for out_ref, first in ((mine_ref, core * half), (other_ref, (1 - core) * half)):
            for v in range(half):
                value = acc_ref[pl.ds(first + v, lags, stride=n), :]
                out_ref[:, v * lags : (v + 1) * lags] = value.T


def correlate(blocks, pieces):
    n = len(blocks)
    lags, width = blocks[0].shape
    k = PIECES * pieces[0].shape[1]
    steps = LE // TAPS
    whole = pl.BlockSpec(memory_space=pltpu.VMEM)
    e_spec = pl.BlockSpec((TAPS, k // PIECES, width), lambda i: (i, 0, 0))
    return pl.pallas_call(
        functools.partial(correlate_kernel, n, steps),
        grid=(steps,),
        in_specs=[whole] * n + [e_spec] * PIECES,
        out_specs=[whole, whole],
        out_shape=[jax.ShapeDtypeStruct((k, n * lags // 2), jnp.float32)] * 2,
        scratch_shapes=[
            pltpu.VMEM((n * lags, k), jnp.float32),
            pltpu.VMEM((width // LANES, (lags + LE) * n, LANES), jnp.float32),
            pltpu.VMEM((width // LANES, (lags + LE) // GROUP, n, LANES), jnp.float32),
            pltpu.VMEM((width // LANES, lags * n, LANES), jnp.float32),
        ],
        compiler_params=pltpu.CompilerParams(vmem_limit_bytes=VMEM),
        cost_estimate=pl.CostEstimate(
            flops=2 * n * lags * LE * width * k,
            bytes_accessed=2 * LE * width * k,
            transcendentals=0,
        ),
    )(*blocks, *pieces)


def per_device(n, records, templates, offsets, masks):
    blocks, pieces = ring_gather(
        records.T, n, lambda piece: embed(templates, offsets, masks, piece)
    )
    mine, other = correlate(blocks, pieces)
    return mine + lax.ppermute(other, "chan", [(0, 1), (1, 0)])


def solution(mesh):
    return jax.shard_map(
        functools.partial(per_device, mesh.shape["blk"]),
        mesh=mesh,
        in_specs=(
            P("chan", ("groups", "blk")),
            P(None, ("groups", "blk"), "chan"),
            P(("groups", "blk"), "chan"),
            P(("groups", "blk"), "chan"),
        ),
        out_specs=P(("groups", "blk"), "chan"),
        check_vma=False,
    )
```

```python
import functools

import jax
import jax.numpy as jnp
from jax import lax
from jax.experimental import pallas as pl
from jax.experimental.pallas import tpu as pltpu
from jax.sharding import PartitionSpec as P

L = 100
LE = 104
SPAN = LE - L
EPS = 1e-06
LANES = 128
PIECES = 4
ROWS = 16
TAPS = 8
TILE = 512
GROUP = 8
EMBED_VMEM = 8 * 1024 * 1024
VMEM = 28 * 1024 * 1024


def embed_kernel(t_ref, place_ref, e_ref):
    rows, cols = place_ref.shape
    for w in range(cols // LANES):
        lanes = slice(w * LANES, (w + 1) * LANES)
        total = jnp.zeros((rows, LANES), jnp.float32)
        for l in range(L):
            v = t_ref[l, :, lanes].astype(jnp.float32)
            total = total + v * v
        scale = lax.rsqrt(total / L + EPS) * (place_ref[:, lanes] >> 3).astype(jnp.float32) / L
        off = place_ref[:, lanes] & 7
        odd = ((off & 1) == 1).astype(jnp.bfloat16) > 0
        high = (off >= 2).astype(jnp.bfloat16) > 0
        full = (off == SPAN).astype(jnp.bfloat16) > 0
        zero = jnp.zeros((rows, LANES), jnp.bfloat16)
        plain = [zero] * SPAN
        moved = [zero] * 2
        for j in range(LE):
            sample = t_ref[j, :, lanes] if j < L else zero
            now = jnp.where(odd, plain[-1], sample)
            value = jnp.where(full, plain[0], jnp.where(high, moved[0], now))
            e_ref[j, :, lanes] = (value.astype(jnp.float32) * scale).astype(jnp.bfloat16)
            plain = plain[1:] + [sample]
            moved = moved[1:] + [now]


def embed(templates, places, piece):
    k, channels = places.shape
    rows = k // PIECES
    steps = rows // ROWS
    first = piece * steps
    width = 2 * LANES
    return pl.pallas_call(
        embed_kernel,
        grid=(steps, channels // width),
        in_specs=[
            pl.BlockSpec((L, ROWS, width), lambda i, j: (0, first + i, j)),
            pl.BlockSpec((ROWS, width), lambda i, j: (first + i, j)),
        ],
        out_specs=pl.BlockSpec((LE, ROWS, width), lambda i, j: (0, i, j)),
        out_shape=jax.ShapeDtypeStruct((LE, rows, channels), jnp.bfloat16),
        compiler_params=pltpu.CompilerParams(vmem_limit_bytes=EMBED_VMEM),
        cost_estimate=pl.CostEstimate(
            flops=20 * LE * rows * channels,
            bytes_accessed=2 * 2 * LE * rows * channels,
            transcendentals=0,
        ),
    )(templates, places)


def ring_position(b, n):
    z, y = b // 2, b % 2
    return z * (1 - y) + (n - 1 - z) * y


def ring_block(p, n):
    half = n // 2
    low = (p < half) * 1 if isinstance(p, int) else (p < half).astype(jnp.int32)
    return low * (2 * p) + (1 - low) * (2 * (n - 1 - p) + 1)


def ring_gather(x, n, beside):
    order = [ring_block(p, n) for p in range(n)]
    up = [(order[p], order[(p + 1) % n]) for p in range(n)]
    down = [(order[(p + 1) % n], order[p]) for p in range(n)]
    blocks = {0: x}
    done = []
    a = b = x
    for step in range(1, n // 2 + 1):
        a = lax.ppermute(a, "blk", up)
        if step < n // 2:
            b = lax.ppermute(b, "blk", down)
        last = step == n // 2
        while step > 1 and len(done) < (PIECES if last else min(step - 1, PIECES)):
            done.append(beside(len(done)))
            a, b, done[-1] = lax.optimization_barrier((a, b, done[-1]))
        blocks[n - step] = a
        if step < n // 2:
            blocks[step] = b
    return [blocks[d] for d in range(n)], done


def prepare(n, block_refs, x_ref, g_ref, n_ref):
    lags, width = block_refs[0].shape
    me = ring_position(lax.axis_index("blk"), n)
    for d in range(n):
        v = ring_block(lax.rem(me + d, n), n)
        for w in range(width // LANES):
            for u in range(0, lags, 16):
                value = block_refs[d][u : u + 16, w * LANES : (w + 1) * LANES].astype(jnp.float32)
                for i in range(2):
                    x_ref[w, pl.ds((u + 8 * i) * n + v, 8, stride=n), :] = value[8 * i : 8 * i + 8]

        @pl.when(v > 0)
        def _():
            for w in range(width // LANES):
                for u in range(0, LE, 8):
                    value = x_ref[w, pl.ds(u * n + v, 8, stride=n), :]
                    x_ref[w, pl.ds((lags + u) * n + v - 1, 8, stride=n), :] = value

        @pl.when(v == 0)
        def _():
            for w in range(width // LANES):
                for u in range(0, LE, 8):
                    x_ref[w, pl.ds((lags + u) * n + n - 1, 8, stride=n), :] = jnp.zeros(
                        (8, LANES), jnp.float32
                    )

    size = GROUP * n

    def energy(g, carry):
        for w in range(width // LANES):
            value = x_ref[w, pl.ds(pl.multiple_of(g * size, size), size), :].reshape(GROUP, n, LANES)
            g_ref[w, g] = jnp.sum(value * value, axis=0)
        return carry

    lax.fori_loop(0, (lags + LE) // GROUP, energy, 0)

    def norms(g, carry):
        for w in range(width // LANES):
            middle = g_ref[w, g + 1]
            for i in range(2, LE // GROUP):
                middle = middle + g_ref[w, g + i]
            left = x_ref[w, pl.ds(pl.multiple_of(g * size, size), size), :].reshape(GROUP, n, LANES)
            right = x_ref[w, pl.ds(pl.multiple_of(g * size + LE * n, size), size), :]
            right = right.reshape(GROUP, n, LANES)
            left = left * left
            right = right * right
            tails = [None] * GROUP
            tail = middle
            for r in range(GROUP - 1, -1, -1):
                tail = tail + left[r]
                tails[r] = tail
            head = None
            for r in range(GROUP):
                total = tails[r]
                if r > 0:
                    head = right[0] if r == 1 else head + right[r - 1]
                    total = total + head
                row = pl.ds(pl.multiple_of((g * GROUP + r) * n, n), n)
                n_ref[w, row, :] = lax.rsqrt(total / LE + EPS)
        return carry

    lax.fori_loop(0, lags // GROUP, norms, 0)


def correlate_kernel(n, steps, *refs):
    blocks = refs[:n]
    e_refs = refs[n : n + PIECES]
    mine_ref, other_ref, acc_ref, x_ref, g_ref, n_ref = refs[n + PIECES :]
    lags, width = blocks[0].shape
    step = pl.program_id(0)

    @pl.when(step == 0)
    def _():
        prepare(n, blocks, x_ref, g_ref, n_ref)
        acc_ref[...] = jnp.zeros_like(acc_ref)

    def tile(m, carry):
        rows = pl.ds(pl.multiple_of(m * TILE, TILE), TILE)
        parts = []
        for tap in range(TAPS):
            first = pl.multiple_of(m * TILE + (step * TAPS + tap) * n, n)
            for w in range(width // LANES):
                value = x_ref[w, pl.ds(first, TILE), :] * n_ref[w, rows, :]
                parts.append(value.astype(jnp.bfloat16))
        windows = jnp.concatenate(parts, axis=1)
        weights = jnp.concatenate(
            [jnp.concatenate([e_ref[tap] for e_ref in e_refs], axis=0) for tap in range(TAPS)],
            axis=1,
        )
        acc_ref[rows, :] += lax.dot_general(
            windows, weights, (((1,), (1,)), ((), ())), preferred_element_type=jnp.float32
        )
        return carry

    lax.fori_loop(0, n * lags // TILE, tile, 0)

    @pl.when(step == steps - 1)
    def _():
        core = lax.axis_index("chan")
        half = n // 2
        for out_ref, first in ((mine_ref, core * half), (other_ref, (1 - core) * half)):
            for v in range(half):
                value = acc_ref[pl.ds(first + v, lags, stride=n), :]
                out_ref[:, v * lags : (v + 1) * lags] = value.T


def correlate(blocks, pieces):
    n = len(blocks)
    lags, width = blocks[0].shape
    k = PIECES * pieces[0].shape[1]
    steps = LE // TAPS
    whole = pl.BlockSpec(memory_space=pltpu.VMEM)
    e_spec = pl.BlockSpec((TAPS, k // PIECES, width), lambda i: (i, 0, 0))
    return pl.pallas_call(
        functools.partial(correlate_kernel, n, steps),
        grid=(steps,),
        in_specs=[whole] * n + [e_spec] * PIECES,
        out_specs=[whole, whole],
        out_shape=[jax.ShapeDtypeStruct((k, n * lags // 2), jnp.float32)] * 2,
        scratch_shapes=[
            pltpu.VMEM((n * lags, k), jnp.float32),
            pltpu.VMEM((width // LANES, (lags + LE) * n, LANES), jnp.float32),
            pltpu.VMEM((width // LANES, (lags + LE) // GROUP, n, LANES), jnp.float32),
            pltpu.VMEM((width // LANES, lags * n, LANES), jnp.float32),
        ],
        compiler_params=pltpu.CompilerParams(vmem_limit_bytes=VMEM),
        cost_estimate=pl.CostEstimate(
            flops=2 * n * lags * LE * width * k,
            bytes_accessed=2 * LE * width * k,
            transcendentals=0,
        ),
    )(*blocks, *pieces)


def per_device(n, records, templates, offsets, masks):
    places = offsets + 8 * masks
    blocks, pieces = ring_gather(records.T, n, lambda piece: embed(templates, places, piece))
    mine, other = correlate(blocks, pieces)
    return mine + lax.ppermute(other, "chan", [(0, 1), (1, 0)])


def solution(mesh):
    return jax.shard_map(
        functools.partial(per_device, mesh.shape["blk"]),
        mesh=mesh,
        in_specs=(
            P("chan", ("groups", "blk")),
            P(None, ("groups", "blk"), "chan"),
            P(("groups", "blk"), "chan"),
            P(("groups", "blk"), "chan"),
        ),
        out_specs=P(("groups", "blk"), "chan"),
        check_vma=False,
    )
```

```python
import functools

import jax
import jax.numpy as jnp
from jax import lax
from jax.experimental import pallas as pl
from jax.experimental.pallas import tpu as pltpu
from jax.sharding import PartitionSpec as P

L = 100
LE = 104
SPAN = LE - L
EPS = 1e-06
LANES = 128
PIECES = 4
ROWS = 16
TAPS = 4
TILE = 1024
GROUP = 8
EMBED_VMEM = 44 * 1024 * 1024
VMEM = 28 * 1024 * 1024


def embed_kernel(t_ref, place_ref, e_ref):
    rows, cols = place_ref.shape
    for w in range(cols // LANES):
        lanes = slice(w * LANES, (w + 1) * LANES)
        total = jnp.zeros((rows, LANES), jnp.float32)
        for l in range(L):
            v = t_ref[l, :, lanes].astype(jnp.float32)
            total = total + v * v
        scale = lax.rsqrt(total / L + EPS) * (place_ref[:, lanes] >> 3).astype(jnp.float32) / L
        off = place_ref[:, lanes] & 7
        odd = ((off & 1) == 1).astype(jnp.bfloat16) > 0
        high = (off >= 2).astype(jnp.bfloat16) > 0
        full = (off == SPAN).astype(jnp.bfloat16) > 0
        zero = jnp.zeros((rows, LANES), jnp.bfloat16)
        plain = [zero] * SPAN
        moved = [zero] * 2
        for j in range(LE):
            sample = t_ref[j, :, lanes] if j < L else zero
            now = jnp.where(odd, plain[-1], sample)
            value = jnp.where(full, plain[0], jnp.where(high, moved[0], now))
            e_ref[j, :, lanes] = (value.astype(jnp.float32) * scale).astype(jnp.bfloat16)
            plain = plain[1:] + [sample]
            moved = moved[1:] + [now]


def embed(templates, places, piece):
    k, channels = places.shape
    rows = k // PIECES
    steps = rows // ROWS
    first = piece * steps
    width = 2 * LANES
    return pl.pallas_call(
        embed_kernel,
        grid=(steps, channels // width),
        in_specs=[
            pl.BlockSpec((L, ROWS, width), lambda i, j: (0, first + i, j)),
            pl.BlockSpec((ROWS, width), lambda i, j: (first + i, j)),
        ],
        out_specs=pl.BlockSpec((LE, ROWS, width), lambda i, j: (0, i, j)),
        out_shape=jax.ShapeDtypeStruct((LE, rows, channels), jnp.bfloat16),
        compiler_params=pltpu.CompilerParams(vmem_limit_bytes=EMBED_VMEM),
        cost_estimate=pl.CostEstimate(
            flops=20 * LE * rows * channels,
            bytes_accessed=2 * 2 * LE * rows * channels,
            transcendentals=0,
        ),
    )(templates, places)


def ring_position(b, n):
    z, y = b // 2, b % 2
    return z * (1 - y) + (n - 1 - z) * y


def ring_block(p, n):
    half = n // 2
    low = (p < half) * 1 if isinstance(p, int) else (p < half).astype(jnp.int32)
    return low * (2 * p) + (1 - low) * (2 * (n - 1 - p) + 1)


def ring_gather(x, n, beside):
    order = [ring_block(p, n) for p in range(n)]
    up = [(order[p], order[(p + 1) % n]) for p in range(n)]
    down = [(order[(p + 1) % n], order[p]) for p in range(n)]
    blocks = {0: x}
    done = []
    a = b = x
    for step in range(1, n // 2 + 1):
        a = lax.ppermute(a, "blk", up)
        if step < n // 2:
            b = lax.ppermute(b, "blk", down)
        if step <= PIECES:
            done.append(beside(step - 1))
            a, b, done[-1] = lax.optimization_barrier((a, b, done[-1]))
        blocks[n - step] = a
        if step < n // 2:
            blocks[step] = b
    return [blocks[d] for d in range(n)], done


def prepare(n, block_refs, x_ref, g_ref, n_ref):
    lags, width = block_refs[0].shape
    me = ring_position(lax.axis_index("blk"), n)
    for d in range(n):
        v = ring_block(lax.rem(me + d, n), n)
        for w in range(width // LANES):
            for u in range(0, lags, 16):
                value = block_refs[d][u : u + 16, w * LANES : (w + 1) * LANES].astype(jnp.float32)
                for i in range(2):
                    x_ref[w, pl.ds((u + 8 * i) * n + v, 8, stride=n), :] = value[8 * i : 8 * i + 8]

        @pl.when(v > 0)
        def _():
            for w in range(width // LANES):
                for u in range(0, LE, 8):
                    value = x_ref[w, pl.ds(u * n + v, 8, stride=n), :]
                    x_ref[w, pl.ds((lags + u) * n + v - 1, 8, stride=n), :] = value

        @pl.when(v == 0)
        def _():
            for w in range(width // LANES):
                for u in range(0, LE, 8):
                    x_ref[w, pl.ds((lags + u) * n + n - 1, 8, stride=n), :] = jnp.zeros(
                        (8, LANES), jnp.float32
                    )

    size = GROUP * n

    def energy(g, carry):
        for w in range(width // LANES):
            value = x_ref[w, pl.ds(pl.multiple_of(g * size, size), size), :].reshape(GROUP, n, LANES)
            g_ref[w, g] = jnp.sum(value * value, axis=0)
        return carry

    lax.fori_loop(0, (lags + LE) // GROUP, energy, 0)

    def norms(g, carry):
        for w in range(width // LANES):
            middle = g_ref[w, g + 1]
            for i in range(2, LE // GROUP):
                middle = middle + g_ref[w, g + i]
            left = x_ref[w, pl.ds(pl.multiple_of(g * size, size), size), :].reshape(GROUP, n, LANES)
            right = x_ref[w, pl.ds(pl.multiple_of(g * size + LE * n, size), size), :]
            right = right.reshape(GROUP, n, LANES)
            left = left * left
            right = right * right
            tails = [None] * GROUP
            tail = middle
            for r in range(GROUP - 1, -1, -1):
                tail = tail + left[r]
                tails[r] = tail
            head = None
            for r in range(GROUP):
                total = tails[r]
                if r > 0:
                    head = right[0] if r == 1 else head + right[r - 1]
                    total = total + head
                row = pl.ds(pl.multiple_of((g * GROUP + r) * n, n), n)
                n_ref[w, row, :] = lax.rsqrt(total / LE + EPS)
        return carry

    lax.fori_loop(0, lags // GROUP, norms, 0)


def correlate_kernel(n, steps, *refs):
    blocks = refs[:n]
    e_refs = refs[n : n + PIECES]
    mine_ref, other_ref, acc_ref, x_ref, g_ref, n_ref = refs[n + PIECES :]
    lags, width = blocks[0].shape
    step = pl.program_id(0)

    @pl.when(step == 0)
    def _():
        prepare(n, blocks, x_ref, g_ref, n_ref)
        acc_ref[...] = jnp.zeros_like(acc_ref)

    def tile(m, carry):
        rows = pl.ds(pl.multiple_of(m * TILE, TILE), TILE)
        parts = []
        for tap in range(TAPS):
            first = pl.multiple_of(m * TILE + (step * TAPS + tap) * n, n)
            for w in range(width // LANES):
                value = x_ref[w, pl.ds(first, TILE), :] * n_ref[w, rows, :]
                parts.append(value.astype(jnp.bfloat16))
        windows = jnp.concatenate(parts, axis=1)
        weights = jnp.concatenate(
            [jnp.concatenate([e_ref[tap] for e_ref in e_refs], axis=0) for tap in range(TAPS)],
            axis=1,
        )
        acc_ref[rows, :] += lax.dot_general(
            windows, weights, (((1,), (1,)), ((), ())), preferred_element_type=jnp.float32
        )
        return carry

    lax.fori_loop(0, n * lags // TILE, tile, 0)

    @pl.when(step == steps - 1)
    def _():
        core = lax.axis_index("chan")
        half = n // 2
        for out_ref, first in ((mine_ref, core * half), (other_ref, (1 - core) * half)):
            for v in range(half):
                value = acc_ref[pl.ds(first + v, lags, stride=n), :]
                out_ref[:, v * lags : (v + 1) * lags] = value.T


def correlate(blocks, pieces):
    n = len(blocks)
    lags, width = blocks[0].shape
    k = PIECES * pieces[0].shape[1]
    steps = LE // TAPS
    whole = pl.BlockSpec(memory_space=pltpu.VMEM)
    e_spec = pl.BlockSpec((TAPS, k // PIECES, width), lambda i: (i, 0, 0))
    return pl.pallas_call(
        functools.partial(correlate_kernel, n, steps),
        grid=(steps,),
        in_specs=[whole] * n + [e_spec] * PIECES,
        out_specs=[whole, whole],
        out_shape=[jax.ShapeDtypeStruct((k, n * lags // 2), jnp.float32)] * 2,
        scratch_shapes=[
            pltpu.VMEM((n * lags, k), jnp.float32),
            pltpu.VMEM((width // LANES, (lags + LE) * n, LANES), jnp.float32),
            pltpu.VMEM((width // LANES, (lags + LE) // GROUP, n, LANES), jnp.float32),
            pltpu.VMEM((width // LANES, lags * n, LANES), jnp.float32),
        ],
        compiler_params=pltpu.CompilerParams(vmem_limit_bytes=VMEM),
        cost_estimate=pl.CostEstimate(
            flops=2 * n * lags * LE * width * k,
            bytes_accessed=2 * LE * width * k,
            transcendentals=0,
        ),
    )(*blocks, *pieces)


def per_device(n, records, templates, offsets, masks):
    places = offsets + 8 * masks
    blocks, pieces = ring_gather(records.T, n, lambda piece: embed(templates, places, piece))
    mine, other = correlate(blocks, pieces)
    return mine + lax.ppermute(other, "chan", [(0, 1), (1, 0)])


def solution(mesh):
    return jax.shard_map(
        functools.partial(per_device, mesh.shape["blk"]),
        mesh=mesh,
        in_specs=(
            P("chan", ("groups", "blk")),
            P(None, ("groups", "blk"), "chan"),
            P(("groups", "blk"), "chan"),
            P(("groups", "blk"), "chan"),
        ),
        out_specs=P(("groups", "blk"), "chan"),
        check_vma=False,
    )
```

```python
import functools

import jax
import jax.numpy as jnp
from jax import lax
from jax.experimental import pallas as pl
from jax.experimental.pallas import tpu as pltpu
from jax.sharding import PartitionSpec as P

L = 100
LE = 104
SPAN = LE - L
EPS = 1e-06
LANES = 128
PIECES = 4
ROWS = 16
TAPS = 4
TILE = 1024
CHUNK = 8
GROUP = 8
EMBED_VMEM = 44 * 1024 * 1024
VMEM = 28 * 1024 * 1024


def embed_kernel(t_ref, place_ref, e_ref):
    rows, cols = place_ref.shape
    for w in range(cols // LANES):
        lanes = slice(w * LANES, (w + 1) * LANES)
        total = jnp.zeros((rows, LANES), jnp.float32)
        for l in range(L):
            v = t_ref[l, :, lanes].astype(jnp.float32)
            total = total + v * v
        scale = lax.rsqrt(total / L + EPS) * (place_ref[:, lanes] >> 3).astype(jnp.float32) / L
        off = place_ref[:, lanes] & 7
        odd = ((off & 1) == 1).astype(jnp.bfloat16) > 0
        high = (off >= 2).astype(jnp.bfloat16) > 0
        full = (off == SPAN).astype(jnp.bfloat16) > 0
        zero = jnp.zeros((rows, LANES), jnp.bfloat16)
        plain = [zero] * SPAN
        moved = [zero] * 2
        for j in range(LE):
            sample = t_ref[j, :, lanes] if j < L else zero
            now = jnp.where(odd, plain[-1], sample)
            value = jnp.where(full, plain[0], jnp.where(high, moved[0], now))
            e_ref[j, :, lanes] = (value.astype(jnp.float32) * scale).astype(jnp.bfloat16)
            plain = plain[1:] + [sample]
            moved = moved[1:] + [now]


def embed(templates, places, piece):
    k, channels = places.shape
    rows = k // PIECES
    steps = rows // ROWS
    first = piece * steps
    width = 2 * LANES
    return pl.pallas_call(
        embed_kernel,
        grid=(steps, channels // width),
        in_specs=[
            pl.BlockSpec((L, ROWS, width), lambda i, j: (0, first + i, j)),
            pl.BlockSpec((ROWS, width), lambda i, j: (first + i, j)),
        ],
        out_specs=pl.BlockSpec((LE, ROWS, width), lambda i, j: (0, i, j)),
        out_shape=jax.ShapeDtypeStruct((LE, rows, channels), jnp.bfloat16),
        compiler_params=pltpu.CompilerParams(vmem_limit_bytes=EMBED_VMEM),
        cost_estimate=pl.CostEstimate(
            flops=20 * LE * rows * channels,
            bytes_accessed=2 * 2 * LE * rows * channels,
            transcendentals=0,
        ),
    )(templates, places)


def ring_position(b, n):
    z, y = b // 2, b % 2
    return z * (1 - y) + (n - 1 - z) * y


def ring_block(p, n):
    half = n // 2
    low = (p < half) * 1 if isinstance(p, int) else (p < half).astype(jnp.int32)
    return low * (2 * p) + (1 - low) * (2 * (n - 1 - p) + 1)


def ring_gather(x, n, beside):
    order = [ring_block(p, n) for p in range(n)]
    up = [(order[p], order[(p + 1) % n]) for p in range(n)]
    down = [(order[(p + 1) % n], order[p]) for p in range(n)]
    blocks = {0: x}
    done = []
    a = b = x
    for step in range(1, n // 2 + 1):
        a = lax.ppermute(a, "blk", up)
        if step < n // 2:
            b = lax.ppermute(b, "blk", down)
        if step <= PIECES:
            done.append(beside(step - 1))
            a, b, done[-1] = lax.optimization_barrier((a, b, done[-1]))
        blocks[n - step] = a
        if step < n // 2:
            blocks[step] = b
    return [blocks[d] for d in range(n)], done


def prepare(n, block_refs, x_ref, g_ref, n_ref):
    lags, width = block_refs[0].shape
    me = ring_position(lax.axis_index("blk"), n)
    for d in range(n):
        v = ring_block(lax.rem(me + d, n), n)
        for w in range(width // LANES):
            for u in range(0, lags, 16):
                value = block_refs[d][u : u + 16, w * LANES : (w + 1) * LANES].astype(jnp.float32)
                for i in range(2):
                    x_ref[w, pl.ds((u + 8 * i) * n + v, 8, stride=n), :] = value[8 * i : 8 * i + 8]

        @pl.when(v > 0)
        def _():
            for w in range(width // LANES):
                for u in range(0, LE, 8):
                    value = x_ref[w, pl.ds(u * n + v, 8, stride=n), :]
                    x_ref[w, pl.ds((lags + u) * n + v - 1, 8, stride=n), :] = value

        @pl.when(v == 0)
        def _():
            for w in range(width // LANES):
                for u in range(0, LE, 8):
                    x_ref[w, pl.ds((lags + u) * n + n - 1, 8, stride=n), :] = jnp.zeros(
                        (8, LANES), jnp.float32
                    )

    size = GROUP * n

    def energy(g, carry):
        for w in range(width // LANES):
            value = x_ref[w, pl.ds(pl.multiple_of(g * size, size), size), :].reshape(GROUP, n, LANES)
            g_ref[w, g] = jnp.sum(value * value, axis=0)
        return carry

    lax.fori_loop(0, (lags + LE) // GROUP, energy, 0)

    def norms(g, carry):
        for w in range(width // LANES):
            middle = g_ref[w, g + 1]
            for i in range(2, LE // GROUP):
                middle = middle + g_ref[w, g + i]
            left = x_ref[w, pl.ds(pl.multiple_of(g * size, size), size), :].reshape(GROUP, n, LANES)
            right = x_ref[w, pl.ds(pl.multiple_of(g * size + LE * n, size), size), :]
            right = right.reshape(GROUP, n, LANES)
            left = left * left
            right = right * right
            tails = [None] * GROUP
            tail = middle
            for r in range(GROUP - 1, -1, -1):
                tail = tail + left[r]
                tails[r] = tail
            head = None
            for r in range(GROUP):
                total = tails[r]
                if r > 0:
                    head = right[0] if r == 1 else head + right[r - 1]
                    total = total + head
                row = pl.ds(pl.multiple_of((g * GROUP + r) * n, n), n)
                n_ref[w, row, :] = lax.rsqrt(total / LE + EPS)
        return carry

    lax.fori_loop(0, lags // GROUP, norms, 0)


def correlate_kernel(n, steps, *refs):
    blocks = refs[:n]
    e_refs = refs[n : n + PIECES]
    mine_ref, other_ref, acc_ref, x_ref, g_ref, n_ref = refs[n + PIECES :]
    lags, width = blocks[0].shape
    step = pl.program_id(0)

    @pl.when(step == 0)
    def _():
        prepare(n, blocks, x_ref, g_ref, n_ref)
        acc_ref[...] = jnp.zeros_like(acc_ref)

    def tile(m, carry):
        rows = pl.ds(pl.multiple_of(m * TILE, TILE), TILE)
        tiles = width // LANES
        parts = [[[] for _ in range(tiles)] for _ in range(TAPS)]
        size = CHUNK * n
        for tap0 in range(0, TAPS, 2):
            for w in range(tiles):
                for c in range(0, TILE, size):
                    first = pl.multiple_of(m * TILE + c, size)
                    norm = n_ref[w, pl.ds(first, size), :]
                    first = pl.multiple_of(first + (step * TAPS + tap0) * n, n)
                    samples = x_ref[w, pl.ds(first, size + n), :]
                    for tap in range(2):
                        value = samples[tap * n : tap * n + size] * norm
                        parts[tap0 + tap][w].append(value.astype(jnp.bfloat16))
        windows = jnp.concatenate(
            [jnp.concatenate(chunks, axis=0) for part in parts for chunks in part], axis=1
        )
        weights = jnp.concatenate(
            [jnp.concatenate([e_ref[tap] for e_ref in e_refs], axis=0) for tap in range(TAPS)],
            axis=1,
        )
        acc_ref[rows, :] += lax.dot_general(
            windows, weights, (((1,), (1,)), ((), ())), preferred_element_type=jnp.float32
        )
        return carry

    lax.fori_loop(0, n * lags // TILE, tile, 0)

    @pl.when(step == steps - 1)
    def _():
        core = lax.axis_index("chan")
        half = n // 2
        for out_ref, first in ((mine_ref, core * half), (other_ref, (1 - core) * half)):
            for v in range(half):
                value = acc_ref[pl.ds(first + v, lags, stride=n), :]
                out_ref[:, v * lags : (v + 1) * lags] = value.T


def correlate(blocks, pieces):
    n = len(blocks)
    lags, width = blocks[0].shape
    k = PIECES * pieces[0].shape[1]
    steps = LE // TAPS
    whole = pl.BlockSpec(memory_space=pltpu.VMEM)
    e_spec = pl.BlockSpec((TAPS, k // PIECES, width), lambda i: (i, 0, 0))
    return pl.pallas_call(
        functools.partial(correlate_kernel, n, steps),
        grid=(steps,),
        in_specs=[whole] * n + [e_spec] * PIECES,
        out_specs=[whole, whole],
        out_shape=[jax.ShapeDtypeStruct((k, n * lags // 2), jnp.float32)] * 2,
        scratch_shapes=[
            pltpu.VMEM((n * lags, k), jnp.float32),
            pltpu.VMEM((width // LANES, (lags + LE) * n, LANES), jnp.float32),
            pltpu.VMEM((width // LANES, (lags + LE) // GROUP, n, LANES), jnp.float32),
            pltpu.VMEM((width // LANES, lags * n, LANES), jnp.float32),
        ],
        compiler_params=pltpu.CompilerParams(vmem_limit_bytes=VMEM),
        cost_estimate=pl.CostEstimate(
            flops=2 * n * lags * LE * width * k,
            bytes_accessed=2 * LE * width * k,
            transcendentals=0,
        ),
    )(*blocks, *pieces)


def per_device(n, records, templates, offsets, masks):
    places = offsets + 8 * masks
    blocks, pieces = ring_gather(records.T, n, lambda piece: embed(templates, places, piece))
    mine, other = correlate(blocks, pieces)
    return mine + lax.ppermute(other, "chan", [(0, 1), (1, 0)])


def solution(mesh):
    return jax.shard_map(
        functools.partial(per_device, mesh.shape["blk"]),
        mesh=mesh,
        in_specs=(
            P("chan", ("groups", "blk")),
            P(None, ("groups", "blk"), "chan"),
            P(("groups", "blk"), "chan"),
            P(("groups", "blk"), "chan"),
        ),
        out_specs=P(("groups", "blk"), "chan"),
        check_vma=False,
    )
```

```python
import functools

import jax
import jax.numpy as jnp
from jax import lax
from jax.experimental import pallas as pl
from jax.experimental.pallas import tpu as pltpu
from jax.sharding import PartitionSpec as P

L = 100
LE = 104
SPAN = LE - L
EPS = 1e-06
LANES = 128
PIECES = 4
ROWS = 16
TAPS = 4
TILE = 1024
GROUP = 8
EMBED_VMEM = 44 * 1024 * 1024
VMEM = 28 * 1024 * 1024


def embed_kernel(t_ref, place_ref, e_ref):
    rows, cols = place_ref.shape
    for w in range(cols // LANES):
        lanes = slice(w * LANES, (w + 1) * LANES)
        total = jnp.zeros((rows, LANES), jnp.float32)
        for l in range(L):
            v = t_ref[l, :, lanes].astype(jnp.float32)
            total = total + v * v
        scale = lax.rsqrt(total / L + EPS) * (place_ref[:, lanes] >> 3).astype(jnp.float32) / L
        off = place_ref[:, lanes] & 7
        odd = ((off & 1) == 1).astype(jnp.bfloat16) > 0
        high = (off >= 2).astype(jnp.bfloat16) > 0
        full = (off == SPAN).astype(jnp.bfloat16) > 0
        zero = jnp.zeros((rows, LANES), jnp.bfloat16)
        plain = [zero] * SPAN
        moved = [zero] * 2
        for j in range(LE):
            sample = t_ref[j, :, lanes] if j < L else zero
            now = jnp.where(odd, plain[-1], sample)
            value = jnp.where(full, plain[0], jnp.where(high, moved[0], now))
            e_ref[j, :, lanes] = (value.astype(jnp.float32) * scale).astype(jnp.bfloat16)
            plain = plain[1:] + [sample]
            moved = moved[1:] + [now]


def embed(templates, places, piece):
    k, channels = places.shape
    rows = k // PIECES
    steps = rows // ROWS
    first = piece * steps
    width = 2 * LANES
    return pl.pallas_call(
        embed_kernel,
        grid=(steps, channels // width),
        in_specs=[
            pl.BlockSpec((L, ROWS, width), lambda i, j: (0, first + i, j)),
            pl.BlockSpec((ROWS, width), lambda i, j: (first + i, j)),
        ],
        out_specs=pl.BlockSpec((LE, ROWS, width), lambda i, j: (0, i, j)),
        out_shape=jax.ShapeDtypeStruct((LE, rows, channels), jnp.bfloat16),
        compiler_params=pltpu.CompilerParams(vmem_limit_bytes=EMBED_VMEM),
        cost_estimate=pl.CostEstimate(
            flops=20 * LE * rows * channels,
            bytes_accessed=2 * 2 * LE * rows * channels,
            transcendentals=0,
        ),
    )(templates, places)


def ring_position(b, n):
    z, y = b // 2, b % 2
    return z * (1 - y) + (n - 1 - z) * y


def ring_block(p, n):
    half = n // 2
    low = (p < half) * 1 if isinstance(p, int) else (p < half).astype(jnp.int32)
    return low * (2 * p) + (1 - low) * (2 * (n - 1 - p) + 1)


def ring_gather(x, n, beside):
    order = [ring_block(p, n) for p in range(n)]
    up = [(order[p], order[(p + 1) % n]) for p in range(n)]
    down = [(order[(p + 1) % n], order[p]) for p in range(n)]
    blocks = {0: x}
    done = []
    a = b = x
    for step in range(1, n // 2 + 1):
        a = lax.ppermute(a, "blk", up)
        if step < n // 2:
            b = lax.ppermute(b, "blk", down)
        if step <= PIECES:
            done.append(beside(step - 1))
            a, b, done[-1] = lax.optimization_barrier((a, b, done[-1]))
        blocks[n - step] = a
        if step < n // 2:
            blocks[step] = b
    return [blocks[d] for d in range(n)], done


def prepare(n, block_refs, x_ref, g_ref, n_ref):
    lags, width = block_refs[0].shape
    me = ring_position(lax.axis_index("blk"), n)
    for d in range(n):
        v = ring_block(lax.rem(me + d, n), n)
        for w in range(width // LANES):
            for u in range(0, lags, 16):
                value = block_refs[d][u : u + 16, w * LANES : (w + 1) * LANES].astype(jnp.float32)
                for i in range(2):
                    x_ref[w, pl.ds((u + 8 * i) * n + v, 8, stride=n), :] = value[8 * i : 8 * i + 8]

    inner = lax.broadcasted_iota(jnp.int32, (n, LANES), 0) < n - 1

    def past(u, carry):
        for w in range(width // LANES):
            value = x_ref[w, pl.ds(pl.multiple_of(u * n, n), n), :]
            value = jnp.where(inner, pltpu.roll(value, n - 1, 0), 0.0)
            x_ref[w, pl.ds(pl.multiple_of((lags + u) * n, n), n), :] = value
        return carry

    lax.fori_loop(0, LE, past, 0, unroll=8)
    size = GROUP * n

    def energy(g, carry):
        for w in range(width // LANES):
            value = x_ref[w, pl.ds(pl.multiple_of(g * size, size), size), :].reshape(GROUP, n, LANES)
            g_ref[w, g] = jnp.sum(value * value, axis=0)
        return carry

    lax.fori_loop(0, (lags + LE) // GROUP, energy, 0)

    def norms(g, carry):
        for w in range(width // LANES):
            middle = g_ref[w, g + 1]
            for i in range(2, LE // GROUP):
                middle = middle + g_ref[w, g + i]
            left = x_ref[w, pl.ds(pl.multiple_of(g * size, size), size), :].reshape(GROUP, n, LANES)
            right = x_ref[w, pl.ds(pl.multiple_of(g * size + LE * n, size), size), :]
            right = right.reshape(GROUP, n, LANES)
            left = left * left
            right = right * right
            tails = [None] * GROUP
            tail = middle
            for r in range(GROUP - 1, -1, -1):
                tail = tail + left[r]
                tails[r] = tail
            head = None
            for r in range(GROUP):
                total = tails[r]
                if r > 0:
                    head = right[0] if r == 1 else head + right[r - 1]
                    total = total + head
                row = pl.ds(pl.multiple_of((g * GROUP + r) * n, n), n)
                n_ref[w, row, :] = lax.rsqrt(total / LE + EPS)
        return carry

    lax.fori_loop(0, lags // GROUP, norms, 0)


def correlate_kernel(n, steps, *refs):
    blocks = refs[:n]
    e_refs = refs[n : n + PIECES]
    mine_ref, other_ref, acc_ref, x_ref, g_ref, n_ref = refs[n + PIECES :]
    lags, width = blocks[0].shape
    step = pl.program_id(0)

    @pl.when(step == 0)
    def _():
        prepare(n, blocks, x_ref, g_ref, n_ref)
        acc_ref[...] = jnp.zeros_like(acc_ref)

    def tile(m, carry):
        rows = pl.ds(pl.multiple_of(m * TILE, TILE), TILE)
        parts = []
        for tap in range(TAPS):
            first = pl.multiple_of(m * TILE + (step * TAPS + tap) * n, n)
            for w in range(width // LANES):
                value = x_ref[w, pl.ds(first, TILE), :] * n_ref[w, rows, :]
                parts.append(value.astype(jnp.bfloat16))
        windows = jnp.concatenate(parts, axis=1)
        weights = jnp.concatenate(
            [jnp.concatenate([e_ref[tap] for e_ref in e_refs], axis=0) for tap in range(TAPS)],
            axis=1,
        )
        acc_ref[rows, :] += lax.dot_general(
            windows, weights, (((1,), (1,)), ((), ())), preferred_element_type=jnp.float32
        )
        return carry

    lax.fori_loop(0, n * lags // TILE, tile, 0)

    @pl.when(step == steps - 1)
    def _():
        core = lax.axis_index("chan")
        half = n // 2
        for out_ref, first in ((mine_ref, core * half), (other_ref, (1 - core) * half)):
            for v in range(half):
                value = acc_ref[pl.ds(first + v, lags, stride=n), :]
                out_ref[:, v * lags : (v + 1) * lags] = value.T


def correlate(blocks, pieces):
    n = len(blocks)
    lags, width = blocks[0].shape
    k = PIECES * pieces[0].shape[1]
    steps = LE // TAPS
    whole = pl.BlockSpec(memory_space=pltpu.VMEM)
    e_spec = pl.BlockSpec((TAPS, k // PIECES, width), lambda i: (i, 0, 0))
    return pl.pallas_call(
        functools.partial(correlate_kernel, n, steps),
        grid=(steps,),
        in_specs=[whole] * n + [e_spec] * PIECES,
        out_specs=[whole, whole],
        out_shape=[jax.ShapeDtypeStruct((k, n * lags // 2), jnp.float32)] * 2,
        scratch_shapes=[
            pltpu.VMEM((n * lags, k), jnp.float32),
            pltpu.VMEM((width // LANES, (lags + LE) * n, LANES), jnp.float32),
            pltpu.VMEM((width // LANES, (lags + LE) // GROUP, n, LANES), jnp.float32),
            pltpu.VMEM((width // LANES, lags * n, LANES), jnp.float32),
        ],
        compiler_params=pltpu.CompilerParams(vmem_limit_bytes=VMEM),
        cost_estimate=pl.CostEstimate(
            flops=2 * n * lags * LE * width * k,
            bytes_accessed=2 * LE * width * k,
            transcendentals=0,
        ),
    )(*blocks, *pieces)


def per_device(n, records, templates, offsets, masks):
    places = offsets + 8 * masks
    blocks, pieces = ring_gather(records.T, n, lambda piece: embed(templates, places, piece))
    mine, other = correlate(blocks, pieces)
    return mine + lax.ppermute(other, "chan", [(0, 1), (1, 0)])


def solution(mesh):
    return jax.shard_map(
        functools.partial(per_device, mesh.shape["blk"]),
        mesh=mesh,
        in_specs=(
            P("chan", ("groups", "blk")),
            P(None, ("groups", "blk"), "chan"),
            P(("groups", "blk"), "chan"),
            P(("groups", "blk"), "chan"),
        ),
        out_specs=P(("groups", "blk"), "chan"),
        check_vma=False,
    )
```

```python
import functools

import jax
import jax.numpy as jnp
from jax import lax
from jax.experimental import pallas as pl
from jax.experimental.pallas import tpu as pltpu
from jax.sharding import PartitionSpec as P

L = 100
LE = 104
SPAN = LE - L
EPS = 1e-06
LANES = 128
PIECES = 4
ROWS = 16
TAPS = 8
TILE = 1024
GROUP = 8
EMBED_VMEM = 44 * 1024 * 1024
VMEM = 28 * 1024 * 1024


def embed_kernel(t_ref, place_ref, e_ref):
    rows, cols = place_ref.shape
    for w in range(cols // LANES):
        lanes = slice(w * LANES, (w + 1) * LANES)
        total = jnp.zeros((rows, LANES), jnp.float32)
        for l in range(L):
            v = t_ref[l, :, lanes].astype(jnp.float32)
            total = total + v * v
        scale = lax.rsqrt(total / L + EPS) * (place_ref[:, lanes] >> 3).astype(jnp.float32) / L
        off = place_ref[:, lanes] & 7
        odd = ((off & 1) == 1).astype(jnp.bfloat16) > 0
        high = (off >= 2).astype(jnp.bfloat16) > 0
        full = (off == SPAN).astype(jnp.bfloat16) > 0
        zero = jnp.zeros((rows, LANES), jnp.bfloat16)
        plain = [zero] * SPAN
        moved = [zero] * 2
        for j in range(LE):
            sample = t_ref[j, :, lanes] if j < L else zero
            now = jnp.where(odd, plain[-1], sample)
            value = jnp.where(full, plain[0], jnp.where(high, moved[0], now))
            e_ref[j, :, lanes] = (value.astype(jnp.float32) * scale).astype(jnp.bfloat16)
            plain = plain[1:] + [sample]
            moved = moved[1:] + [now]


def embed(templates, places, piece):
    k, channels = places.shape
    rows = k // PIECES
    steps = rows // ROWS
    first = piece * steps
    width = 2 * LANES
    return pl.pallas_call(
        embed_kernel,
        grid=(steps, channels // width),
        in_specs=[
            pl.BlockSpec((L, ROWS, width), lambda i, j: (0, first + i, j)),
            pl.BlockSpec((ROWS, width), lambda i, j: (first + i, j)),
        ],
        out_specs=pl.BlockSpec((LE, ROWS, width), lambda i, j: (0, i, j)),
        out_shape=jax.ShapeDtypeStruct((LE, rows, channels), jnp.bfloat16),
        compiler_params=pltpu.CompilerParams(vmem_limit_bytes=EMBED_VMEM),
        cost_estimate=pl.CostEstimate(
            flops=20 * LE * rows * channels,
            bytes_accessed=2 * 2 * LE * rows * channels,
            transcendentals=0,
        ),
    )(templates, places)


def ring_position(b, n):
    z, y = b // 2, b % 2
    return z * (1 - y) + (n - 1 - z) * y


def ring_block(p, n):
    half = n // 2
    low = (p < half) * 1 if isinstance(p, int) else (p < half).astype(jnp.int32)
    return low * (2 * p) + (1 - low) * (2 * (n - 1 - p) + 1)


def ring_gather(x, n, beside):
    order = [ring_block(p, n) for p in range(n)]
    up = [(order[p], order[(p + 1) % n]) for p in range(n)]
    down = [(order[(p + 1) % n], order[p]) for p in range(n)]
    blocks = {0: x}
    done = []
    a = b = x
    for step in range(1, n // 2 + 1):
        a = lax.ppermute(a, "blk", up)
        if step < n // 2:
            b = lax.ppermute(b, "blk", down)
        if step <= PIECES:
            done.append(beside(step - 1))
            a, b, done[-1] = lax.optimization_barrier((a, b, done[-1]))
        blocks[n - step] = a
        if step < n // 2:
            blocks[step] = b
    return [blocks[d] for d in range(n)], done


def prepare(n, block_refs, x_ref, g_ref, n_ref):
    lags, width = block_refs[0].shape
    me = ring_position(lax.axis_index("blk"), n)
    for d in range(n):
        v = ring_block(lax.rem(me + d, n), n)
        for w in range(width // LANES):
            for u in range(0, lags, 16):
                value = block_refs[d][u : u + 16, w * LANES : (w + 1) * LANES].astype(jnp.float32)
                for i in range(2):
                    x_ref[w, pl.ds((u + 8 * i) * n + v, 8, stride=n), :] = value[8 * i : 8 * i + 8]

    inner = lax.broadcasted_iota(jnp.int32, (n, LANES), 0) < n - 1

    def past(u, carry):
        for w in range(width // LANES):
            value = x_ref[w, pl.ds(pl.multiple_of(u * n, n), n), :]
            value = jnp.where(inner, pltpu.roll(value, n - 1, 0), 0.0)
            x_ref[w, pl.ds(pl.multiple_of((lags + u) * n, n), n), :] = value
        return carry

    lax.fori_loop(0, LE, past, 0, unroll=8)
    size = GROUP * n

    def energy(g, carry):
        for w in range(width // LANES):
            value = x_ref[w, pl.ds(pl.multiple_of(g * size, size), size), :].reshape(GROUP, n, LANES)
            g_ref[w, g] = jnp.sum(value * value, axis=0)
        return carry

    lax.fori_loop(0, (lags + LE) // GROUP, energy, 0)

    def norms(g, carry):
        for w in range(width // LANES):
            middle = g_ref[w, g + 1]
            for i in range(2, LE // GROUP):
                middle = middle + g_ref[w, g + i]
            left = x_ref[w, pl.ds(pl.multiple_of(g * size, size), size), :].reshape(GROUP, n, LANES)
            right = x_ref[w, pl.ds(pl.multiple_of(g * size + LE * n, size), size), :]
            right = right.reshape(GROUP, n, LANES)
            left = left * left
            right = right * right
            tails = [None] * GROUP
            tail = middle
            for r in range(GROUP - 1, -1, -1):
                tail = tail + left[r]
                tails[r] = tail
            head = None
            for r in range(GROUP):
                total = tails[r]
                if r > 0:
                    head = right[0] if r == 1 else head + right[r - 1]
                    total = total + head
                row = pl.ds(pl.multiple_of((g * GROUP + r) * n, n), n)
                n_ref[w, row, :] = lax.rsqrt(total / LE + EPS)
        return carry

    lax.fori_loop(0, lags // GROUP, norms, 0)


def correlate_kernel(n, steps, *refs):
    blocks = refs[:n]
    e_refs = refs[n : n + PIECES]
    mine_ref, other_ref, acc_ref, x_ref, g_ref, n_ref = refs[n + PIECES :]
    lags, width = blocks[0].shape
    step = pl.program_id(0)

    @pl.when(step == 0)
    def _():
        prepare(n, blocks, x_ref, g_ref, n_ref)
        acc_ref[...] = jnp.zeros_like(acc_ref)

    def tile(m, carry):
        rows = pl.ds(pl.multiple_of(m * TILE, TILE), TILE)
        parts = []
        for tap in range(TAPS):
            first = pl.multiple_of(m * TILE + (step * TAPS + tap) * n, n)
            for w in range(width // LANES):
                value = x_ref[w, pl.ds(first, TILE), :] * n_ref[w, rows, :]
                parts.append(value.astype(jnp.bfloat16))
        windows = jnp.concatenate(parts, axis=1)
        weights = jnp.concatenate(
            [jnp.concatenate([e_ref[tap] for e_ref in e_refs], axis=0) for tap in range(TAPS)],
            axis=1,
        )
        acc_ref[rows, :] += lax.dot_general(
            windows, weights, (((1,), (1,)), ((), ())), preferred_element_type=jnp.float32
        )
        return carry

    lax.fori_loop(0, n * lags // TILE, tile, 0)

    @pl.when(step == steps - 1)
    def _():
        core = lax.axis_index("chan")
        half = n // 2
        for out_ref, first in ((mine_ref, core * half), (other_ref, (1 - core) * half)):
            for v in range(half):
                value = acc_ref[pl.ds(first + v, lags, stride=n), :]
                out_ref[:, v * lags : (v + 1) * lags] = value.T


def correlate(blocks, pieces):
    n = len(blocks)
    lags, width = blocks[0].shape
    k = PIECES * pieces[0].shape[1]
    steps = LE // TAPS
    whole = pl.BlockSpec(memory_space=pltpu.VMEM)
    e_spec = pl.BlockSpec((TAPS, k // PIECES, width), lambda i: (i, 0, 0))
    return pl.pallas_call(
        functools.partial(correlate_kernel, n, steps),
        grid=(steps,),
        in_specs=[whole] * n + [e_spec] * PIECES,
        out_specs=[whole, whole],
        out_shape=[jax.ShapeDtypeStruct((k, n * lags // 2), jnp.float32)] * 2,
        scratch_shapes=[
            pltpu.VMEM((n * lags, k), jnp.float32),
            pltpu.VMEM((width // LANES, (lags + LE) * n, LANES), jnp.float32),
            pltpu.VMEM((width // LANES, (lags + LE) // GROUP, n, LANES), jnp.float32),
            pltpu.VMEM((width // LANES, lags * n, LANES), jnp.float32),
        ],
        compiler_params=pltpu.CompilerParams(vmem_limit_bytes=VMEM),
        cost_estimate=pl.CostEstimate(
            flops=2 * n * lags * LE * width * k,
            bytes_accessed=2 * LE * width * k,
            transcendentals=0,
        ),
    )(*blocks, *pieces)


def per_device(n, records, templates, offsets, masks):
    places = offsets + 8 * masks
    blocks, pieces = ring_gather(records.T, n, lambda piece: embed(templates, places, piece))
    mine, other = correlate(blocks, pieces)
    return mine + lax.ppermute(other, "chan", [(0, 1), (1, 0)])


def solution(mesh):
    return jax.shard_map(
        functools.partial(per_device, mesh.shape["blk"]),
        mesh=mesh,
        in_specs=(
            P("chan", ("groups", "blk")),
            P(None, ("groups", "blk"), "chan"),
            P(("groups", "blk"), "chan"),
            P(("groups", "blk"), "chan"),
        ),
        out_specs=P(("groups", "blk"), "chan"),
        check_vma=False,
    )
```
